32 devices in a mesh: lr: 8 (over y, x, core), lc: 4 (over z).
Axes of the slice: x: 2, y: 2, z: 4, core: 2. Of those that a mesh axis runs over, the one named last changes fastest.
Arguments:
- queries: bfloat16 [2048, 768], P(('lr', 'lc')), may hold values from -6 to 6
- probes: int32 [2048, 16], P(('lr', 'lc')), may hold values from 0 to 255, as said below
- assign: int32 [2048], P(('lr', 'lc')), may hold values from 0 to 255, as said below
- list_rows: bfloat16 [256, 1024, 768], P(('lr', 'lc')), may hold values from -0.21875 to 0.21875
- list_fill: int32 [256], P(('lr', 'lc')), may hold values from 1 to 1024
- centroids: float32 [256, 768], P(('lr', 'lc')), may hold values from -6 to 6
- list_sums: float32 [256, 768], P(('lr', 'lc')), may hold values from -6 to 6
Outputs:
- dup_max: float32 [2048, 16], P(('lr', 'lc'))
- codes: bfloat16 [256, 16, 768], P(('lr', 'lc'))
- scales: float32 [256, 16], P(('lr', 'lc'))
- new_sums: float32 [256, 768], P(('lr', 'lc'))
The draws below stay inside these ranges and needn't reach their ends.
Inputs may be any that keep to these rules, and one draw needn't show every extreme that they name: A list id is 8 times its owner's device index along lr+lc plus its place there. The probe pairs of one device's new vectors name lists of one owner at most 64 times, and one list is named by at most 256 pairs over all new vectors; both bounds are reached. A vector's probes may repeat a list. `assign`: one device's new vectors go to lists of one owner at most 4 times, and one list receives at most 16 new vectors; both bounds are reached.
All inputs are finite; a program needn't handle non-finite values. Where the reference program divides by a largest or mean magnitude, that divisor is 1e-20 or more.
Results may differ from the reference program's by a relative error of at most 0.001.
Values may be sent and summed in bfloat16 or wider, within the bound.
No kernel may reach another device: no remote copies, remote signals or barrier semaphores. Data moves between devices by JAX's collectives and lax.ppermute only.
A program may use at most 64 MiB of HBM per device.

```python
import jax
import jax.numpy as jnp
from jax import lax

D = 768
PROBES = 16
Q_DEV = 64
L_DEV = 8
ROWS = 1024
QUERIES = 2048
LISTS = 256
CAP = 64
CAP2 = 4
LIST_CAP = 256
APPEND = 16


def route_draw(key, device_count, item_count, capacity, list_count):
    hot_owner = jax.random.randint(jax.random.fold_in(key, 1), (), 0, device_count).astype(jnp.int32)
    offsets = jax.random.randint(jax.random.fold_in(key, 2), (device_count,), 0, list_count).astype(jnp.int32)

    def one_sender(sender):
        sender_key = jax.random.fold_in(jax.random.fold_in(key, 3), sender)
        shuffled = jax.random.permutation(jax.random.fold_in(sender_key, 4), (device_count - 1) * capacity).astype(jnp.int32)
        chosen = jnp.concatenate([jnp.arange(capacity, dtype=jnp.int32), shuffled[:item_count - capacity] + capacity])
        owner_rank = chosen // capacity
        other_index = owner_rank - 1
        others = other_index + (other_index >= hot_owner).astype(jnp.int32)
        owners = jnp.where(owner_rank == 0, hot_owner, others)
        within = chosen % capacity
        local_ids = (sender * capacity + within + offsets[owners]) % list_count
        list_ids = owners * list_count + local_ids
        reorder = jax.random.permutation(jax.random.fold_in(sender_key, 5), item_count)
        return list_ids[reorder].astype(jnp.int32)
    return jax.vmap(one_sender)(jnp.arange(device_count, dtype=jnp.int32))


def draw_probes(key, part):
    list_ids = route_draw(key, QUERIES // Q_DEV, Q_DEV * PROBES, CAP, L_DEV)
    return list_ids.reshape(QUERIES, PROBES)


def draw_assign(key, part):
    list_ids = route_draw(jax.random.fold_in(key, 7), QUERIES // Q_DEV, Q_DEV, CAP2, L_DEV)
    return list_ids.reshape(QUERIES)


def touch_ends(drawn, key, low, largest):
    index_at = [jax.random.randint(jax.random.fold_in(key, axis), (), 0, length) for axis, length in enumerate(drawn.shape)]
    longest = drawn.shape.index(max(drawn.shape))
    beside = index_at[:longest] + [(index_at[longest] + 1) % drawn.shape[longest]] + index_at[longest + 1:]
    return drawn.at[tuple(index_at)].set(low).at[tuple(beside)].set(largest)


def block_levels(key, shape, shards, low, largest):
    gain, own = 1.0, jax.random.fold_in(key, 6)
    for dim, parts in shards:
        draws = jnp.exp(jax.random.uniform(jax.random.fold_in(own, dim), (parts,), jnp.float32, low / len(shards), largest / len(shards)))
        gain = gain * jnp.repeat(draws, shape[dim] // parts).reshape([-1 if axis == dim else 1 for axis in range(len(shape))])
    return gain


def bell_draw(own_key, extent, spread, most, cuts=(), held_as=jnp.bfloat16):
    array = spread * jax.random.normal(own_key, extent, jnp.float32)
    if cuts:
        array = array * block_levels(own_key, extent, cuts, -0.22, 0.18)
    return jnp.clip(array, -most, most).astype(held_as)


def setup_inputs(seed: int = 0) -> dict:
    streams_of = jax.random.split(jax.random.key(seed), 8)
    queries = bell_draw(streams_of[0], (QUERIES, D), 1.0, 6.0, ((0, 32),))
    probes = draw_probes(jax.random.fold_in(streams_of[7], 71), 0)
    assign = draw_assign(jax.random.fold_in(streams_of[7], 71), 0)
    list_rows = bell_draw(streams_of[3], (LISTS, ROWS, D), D ** -0.5, 0.21875, ((0, 32),))
    list_fill = touch_ends(jax.random.randint(streams_of[4], (LISTS,), 1, ROWS + 1), jax.random.fold_in(streams_of[4], 1), 1, ROWS).astype(jnp.int32)
    centroids = bell_draw(streams_of[5], (LISTS, D), 1.0, 6.0, ((0, 32),), jnp.float32)
    list_sums = bell_draw(streams_of[6], (LISTS, D), 1.0, 6.0, ((0, 32),), jnp.float32)
    return dict(queries=queries, probes=probes, assign=assign, list_rows=list_rows, list_fill=list_fill, centroids=centroids, list_sums=list_sums)


def reference(queries, probes, assign, list_rows, list_fill, centroids, list_sums):
    pair_ids = probes.reshape(-1).astype(jnp.int32)
    pair_total = pair_ids.shape[0]
    sorted_order = jnp.argsort(pair_ids, stable=True).astype(jnp.int32)
    list_counts = jax.ops.segment_sum(jnp.ones_like(pair_ids), pair_ids, num_segments=LISTS).astype(jnp.int32)
    list_starts = (jnp.cumsum(list_counts) - list_counts).astype(jnp.int32)
    padded_order = jnp.concatenate([sorted_order, jnp.zeros((LIST_CAP,), jnp.int32)])

    def score_list(list_id):
        pair_index = lax.dynamic_slice_in_dim(padded_order, list_starts[list_id], LIST_CAP)
        live_slots = jnp.arange(LIST_CAP, dtype=jnp.int32) < list_counts[list_id]
        query_rows = queries[pair_index // PROBES]
        stored = list_rows[list_id]
        scores = jnp.dot(query_rows, stored.T, preferred_element_type=jnp.float32)
        scores = jnp.where(jnp.arange(ROWS, dtype=jnp.int32)[None, :] < list_fill[list_id], scores, -jnp.inf)
        best_scores = jnp.max(scores, axis=1)
        targets = jnp.where(live_slots, pair_index, pair_total).astype(jnp.int32)
        return best_scores, targets

    best_scores, targets = lax.map(score_list, jnp.arange(LISTS, dtype=jnp.int32))
    flat_best = jnp.zeros((pair_total,), jnp.float32).at[targets.reshape(-1)].set(best_scores.reshape(-1), mode="drop")
    dup_max = flat_best.reshape(QUERIES, PROBES)

    list_of = assign.astype(jnp.int32)
    residual = queries.astype(jnp.float32) - centroids[list_of]
    scale = jnp.max(jnp.abs(residual), axis=1) + 1e-6
    code_rows = (residual / scale[:, None]).astype(jnp.bfloat16)
    assign_order = jnp.argsort(list_of, stable=True).astype(jnp.int32)
    assign_counts = jax.ops.segment_sum(jnp.ones_like(list_of), list_of, num_segments=LISTS).astype(jnp.int32)
    assign_starts = (jnp.cumsum(assign_counts) - assign_counts).astype(jnp.int32)
    sorted_slot = jnp.arange(QUERIES, dtype=jnp.int32) - assign_starts[list_of[assign_order]]
    slot = jnp.zeros((QUERIES,), jnp.int32).at[assign_order].set(sorted_slot.astype(jnp.int32))
    position = list_of * APPEND + slot
    codes = jnp.zeros((LISTS * APPEND, D), jnp.bfloat16).at[position].set(code_rows).reshape(LISTS, APPEND, D)
    scales = jnp.zeros((LISTS * APPEND,), jnp.float32).at[position].set(scale).reshape(LISTS, APPEND)
    new_sums = list_sums + jax.ops.segment_sum(residual, list_of, num_segments=LISTS)
    return (dup_max, codes, scales, new_sums)
```

```python
import functools

import jax
import jax.numpy as jnp
from jax import lax
from jax.experimental import pallas as pl
from jax.experimental.pallas import tpu as pltpu
from jax.sharding import PartitionSpec as P

AXES = ("lr", "lc")
VMEM = pl.BlockSpec(memory_space=pltpu.VMEM)
SMEM = pl.BlockSpec(memory_space=pltpu.SMEM)
BF16 = jnp.bfloat16
F32 = jnp.float32


def call(body, out_shape, *args, specs, name, scratch=(), flops=0, limit=24, alias=None):
    many = isinstance(out_shape, (list, tuple))
    return pl.pallas_call(
        body,
        in_specs=list(specs),
        out_specs=[VMEM] * len(out_shape) if many else VMEM,
        out_shape=out_shape,
        scratch_shapes=list(scratch),
        input_output_aliases=alias or {},
        compiler_params=pltpu.CompilerParams(vmem_limit_bytes=limit * 2**20),
        cost_estimate=pl.CostEstimate(flops=flops, bytes_accessed=2**20, transcendentals=0),
        name=name,
    )(*args)


def iota(shape, dim):
    return lax.broadcasted_iota(jnp.int32, shape, dim)


def mark_body(ids_ref, out_ref):
    lists = iota(out_ref.shape, 0)
    hit = lists == ids_ref[0:1, :]
    for j in range(1, ids_ref.shape[0]):
        hit = hit | (lists == ids_ref[j : j + 1, :])
    out_ref[...] = hit.astype(F32)


def rank_body(list_count, marks_ref, out_ref):
    rows, width = marks_ref.shape
    half = width // 2
    marks = marks_ref[...]
    a, b = iota((width, width), 0), iota((width, width), 1)
    same = (a // half) == (b // half)
    earlier = jnp.where(same & (a < b), 1.0, 0.0).astype(BF16)
    every = jnp.where(same, 1.0, 0.0).astype(BF16)
    r, s = iota((rows, rows), 0), iota((rows, rows), 1)
    before = jnp.where((r % list_count == s % list_count) & (s < r), 1.0, 0.0).astype(BF16)
    within = jnp.dot(marks.astype(BF16), earlier, preferred_element_type=F32)
    counts = jnp.dot(marks.astype(BF16), every, preferred_element_type=F32)
    base = jnp.dot(before, counts.astype(BF16), preferred_element_type=F32)
    out_ref[...] = jnp.where(marks > 0.5, within + base, -1.0).astype(jnp.int32)


def pair_ranks(ranks_ref, src_ref, first, list_count, half, part):
    blocks = []
    for i in range(2):
        start = pl.multiple_of(src_ref[first + i] * list_count, list_count)
        block = ranks_ref[pl.ds(start, list_count), :]
        blocks.append(block if i == part else pltpu.roll(block, half, 1))
    lane = iota(blocks[0].shape, 1)
    return jnp.where(lane < half, blocks[0], blocks[1])


def group_body(list_count, per_list, first_piece, has_in, *refs):
    src_ref, ranks_ref = refs[0], refs[1]
    refs = refs[2:]
    if has_in:
        in_ref, refs = refs[0], refs[1:]
    q_refs, out_ref, pick = refs[:-2], refs[-2], refs[-1]
    half = ranks_ref.shape[1] // 2
    depth = pick.shape[1]
    lists_a_step = pick.shape[0] // per_list
    pairs = []
    for p in range(depth // (2 * half)):
        pairs.append(pair_ranks(ranks_ref, src_ref, first_piece + 2 * p, list_count, half, 0))
    place = iota((per_list, 2 * half), 0)
    for step in range(list_count // lists_a_step):
        for i in range(lists_a_step):
            l = step * lists_a_step + i
            for p, ranks in enumerate(pairs):
                pick[i * per_list : (i + 1) * per_list, p * 2 * half : (p + 1) * 2 * half] = jnp.where(
                    ranks[l : l + 1, :] == place, 1.0, 0.0
                ).astype(BF16)
        total = None
        at = 0
        for q_ref in q_refs:
            n = q_ref.shape[0]
            term = jnp.dot(pick[:, at : at + n], q_ref[...], preferred_element_type=F32)
            total = term if total is None else total + term
            at += n
        rows = slice(step * lists_a_step * per_list, (step + 1) * lists_a_step * per_list)
        total = total.astype(BF16)
        out_ref[rows, :] = total + in_ref[rows, :] if has_in else total


def score_body(per_list, fill_ref, ranks_ref, grouped_ref, rows_ref, out_ref, best):
    list_count, row_count, _ = rows_ref.shape
    senders, _, width = out_ref.shape
    for l in range(list_count):
        scores = lax.dot_general(
            rows_ref[l],
            grouped_ref[l * per_list : (l + 1) * per_list, :],
            (((1,), (1,)), ((), ())),
            preferred_element_type=F32,
        )
        scores = jnp.where(iota(scores.shape, 0) < fill_ref[l], scores, -jnp.inf)
        best[l : l + 1, :] = jnp.max(scores, axis=0, keepdims=True)
    for s in range(senders):
        ranks = ranks_ref[s * list_count : (s + 1) * list_count, :]
        found = jnp.zeros(ranks.shape, F32)
        for c in range(per_list // width):
            index = jnp.clip(ranks - c * width, 0, width - 1)
            got = jnp.take_along_axis(best[:, c * width : (c + 1) * width], index, axis=1)
            found = jnp.where((ranks >= c * width) & (ranks < (c + 1) * width), got, found)
        out_ref[s] = found


def pick_body(got_ref, ids_ref, out_ref):
    probe_count = ids_ref.shape[0]
    lists = iota(got_ref.shape, 0)
    got = got_ref[...]
    rows = []
    for j in range(probe_count):
        rows.append(jnp.sum(jnp.where(lists == ids_ref[j : j + 1, :], got, 0.0), axis=0, keepdims=True))
    found = jnp.concatenate(rows, axis=0)
    out_ref[...] = found.T[: out_ref.shape[0], :]


def append_body(list_count, slots, src_ref, ranks_ref, center_ref, sums_ref, *refs):
    q_refs, (codes_ref, scales_ref, sums_out_ref, pick) = refs[:-4], refs[-4:]
    half = ranks_ref.shape[1] // 2
    dim = center_ref.shape[1]
    place = iota((slots, 2 * half), 0)
    piece = 0
    total = jnp.zeros((list_count * slots, dim), F32)
    live = jnp.zeros((list_count * slots, 1), F32)
    for q_ref in q_refs:
        n = q_ref.shape[0]
        for p in range(n // (2 * half)):
            ranks = pair_ranks(ranks_ref, src_ref, piece, list_count, half, 1)
            piece += 2
            for l in range(list_count):
                hit = jnp.where(ranks[l : l + 1, :] == place, 1.0, 0.0)
                pick[l * slots : (l + 1) * slots, p * 2 * half : (p + 1) * 2 * half] = hit.astype(BF16)
        chosen = pick[:, :n]
        live = live + jnp.sum(chosen.astype(F32), axis=1, keepdims=True)
        total = total + jnp.dot(chosen, q_ref[...], preferred_element_type=F32)
    for l in range(list_count):
        rows = slice(l * slots, (l + 1) * slots)
        used = live[rows, :] > 0.5
        residual = jnp.where(used, total[rows, :] - center_ref[l : l + 1, :], 0.0)
        scale = jnp.max(jnp.abs(residual), axis=1, keepdims=True) + 1e-6
        codes_ref[l] = (residual / scale).astype(BF16)
        scales_ref[l : l + 1, :] = jnp.where(used, scale, 0.0).T
        sums_out_ref[l : l + 1, :] = sums_ref[l : l + 1, :] + jnp.sum(residual, axis=0, keepdims=True)


def swap_pairs(rows, cols, of):
    pairs = []
    for lr in range(rows):
        for lc in range(cols):
            to = of(lr, lc)
            pairs.append((lr * cols + lc, to[0] * cols + to[1]))
    return pairs


def gather_queries(queries, rows, cols):
    if (rows, cols) != (8, 4):
        whole = lax.all_gather(queries, AXES, axis=0, tiled=True)
        half = whole.shape[0] // 2
        return [whole[:half], whole[half:]], jnp.arange(rows * cols, dtype=jnp.int32)

    def send(x, of):
        return lax.ppermute(x, AXES, swap_pairs(rows, cols, of))

    def plane(x):
        x = jnp.concatenate([x, send(x, lambda r, c: (r ^ (4 if r & 1 else 2), c))], 0)
        x = jnp.concatenate([x, send(x, lambda r, c: (r ^ (2 if r & 1 else 4), c))], 0)
        return [x, send(x, lambda r, c: (r ^ 1, c))]

    z = [queries] + [send(queries, lambda r, c, k=k: (r, c ^ k)) for k in (1, 2, 3)]
    chunks = plane(jnp.concatenate(z[:2], 0)) + plane(jnp.concatenate(z[2:], 0))
    r, c = lax.axis_index("lr"), lax.axis_index("lc")
    sources = []
    for base in (0, 2):
        for core in (0, 1):
            odd = (r ^ core) & 1
            one, two = jnp.where(odd == 1, 4, 2), jnp.where(odd == 1, 2, 4)
            for piece in range(8):
                row = r ^ core
                row = row ^ one if piece & 2 else row
                row = row ^ two if piece & 4 else row
                sources.append(row * cols + (c ^ (base + (piece & 1))))
    return chunks, jnp.stack(sources).astype(jnp.int32)


def local(queries, probes, assign, list_rows, list_fill, centroids, list_sums):
    rows, cols = lax.axis_size("lr"), lax.axis_size("lc")
    group = rows * cols
    list_count, row_count, dim = list_rows.shape
    query_count, probe_count = probes.shape
    pair_cap = 2 * query_count * probe_count // group
    append_cap = max(2, 2 * query_count // group)
    per_list = group * pair_cap // list_count
    slots = group * append_cap // list_count
    width = 2 * query_count
    total_lists = group * list_count

    chunks, sources = gather_queries(queries, rows, cols)

    probe_ids = probes.T
    ids = jnp.concatenate(
        [probe_ids, jnp.broadcast_to(assign[None, :], (probe_count, query_count))], axis=1
    )
    marks = call(
        mark_body,
        jax.ShapeDtypeStruct((total_lists, width), F32),
        ids,
        specs=[VMEM],
        name="mark",
    )
    marks = lax.all_to_all(
        marks.reshape(group, list_count, width), AXES, split_axis=0, concat_axis=0, tiled=True
    ).reshape(total_lists, width)
    ranks = call(
        functools.partial(rank_body, list_count),
        jax.ShapeDtypeStruct((total_lists, width), jnp.int32),
        marks,
        specs=[VMEM],
        name="rank",
    )

    grouped = None
    first = 0
    half = len(chunks) // 2
    for part in (chunks[:half], chunks[half:]):
        depth = sum(x.shape[0] for x in part)
        has_in = grouped is not None
        grouped = call(
            functools.partial(group_body, list_count, per_list, first, has_in),
            jax.ShapeDtypeStruct((list_count * per_list, dim), BF16),
            sources,
            ranks,
            *([grouped] if has_in else []),
            *part,
            specs=[SMEM] + [VMEM] * (1 + has_in + len(part)),
            scratch=[pltpu.VMEM((2 * per_list, depth), BF16)],
            flops=2 * list_count * per_list * depth * dim,
            limit=28,
            name="group",
        )
        first += depth // query_count

    best = call(
        functools.partial(score_body, per_list),
        jax.ShapeDtypeStruct((group, list_count, width), F32),
        list_fill,
        ranks,
        grouped,
        list_rows,
        specs=[SMEM, VMEM, VMEM, VMEM],
        scratch=[pltpu.VMEM((list_count, per_list), F32)],
        flops=2 * list_count * per_list * row_count * dim,
        name="score",
    )
    got = lax.all_to_all(best, AXES, split_axis=0, concat_axis=0, tiled=True)
    dup_max = call(
        pick_body,
        jax.ShapeDtypeStruct((query_count, probe_count), F32),
        got.reshape(total_lists, width),
        ids,
        specs=[VMEM, VMEM],
        name="pick",
    )

    codes, scales, new_sums = call(
        functools.partial(append_body, list_count, slots),
        [
            jax.ShapeDtypeStruct((list_count, slots, dim), BF16),
            jax.ShapeDtypeStruct((list_count, slots), F32),
            jax.ShapeDtypeStruct((list_count, dim), F32),
        ],
        sources,
        ranks,
        centroids,
        list_sums,
        *chunks,
        specs=[SMEM] + [VMEM] * (3 + len(chunks)),
        scratch=[pltpu.VMEM((list_count * slots, max(x.shape[0] for x in chunks)), BF16)],
        flops=2 * list_count * slots * group * query_count * dim,
        name="append",
    )
    return dup_max, codes, scales, new_sums


def solution(mesh):
    split = P(AXES, None)
    return jax.shard_map(
        local,
        mesh=mesh,
        in_specs=(split, split, P(AXES), P(AXES, None, None), P(AXES), split, split),
        out_specs=(split, P(AXES, None, None), split, split),
        check_vma=False,
    )
```

```python
import functools

import jax
import jax.numpy as jnp
from jax import lax
from jax.experimental import pallas as pl
from jax.experimental.pallas import tpu as pltpu
from jax.sharding import PartitionSpec as P

AXES = ("lr", "lc")
VMEM = pl.BlockSpec(memory_space=pltpu.VMEM)
SMEM = pl.BlockSpec(memory_space=pltpu.SMEM)
BF16 = jnp.bfloat16
F32 = jnp.float32


def call(body, out_shape, *args, specs, name, scratch=(), flops=0, limit=24, alias=None):
    many = isinstance(out_shape, (list, tuple))
    return pl.pallas_call(
        body,
        in_specs=list(specs),
        out_specs=[VMEM] * len(out_shape) if many else VMEM,
        out_shape=out_shape,
        scratch_shapes=list(scratch),
        input_output_aliases=alias or {},
        compiler_params=pltpu.CompilerParams(vmem_limit_bytes=limit * 2**20),
        cost_estimate=pl.CostEstimate(flops=flops, bytes_accessed=0, transcendentals=0),
        name=name,
    )(*args)


def iota(shape, dim):
    return lax.broadcasted_iota(jnp.int32, shape, dim)


def unpack(q_refs, src_ref, first, list_count, id_rows, dim, marks_ref):
    half = marks_ref.shape[1] // 2
    me = src_ref[src_ref.shape[0] - 1]
    marks_ref[...] = jnp.zeros(marks_ref.shape, F32)
    lists = iota((list_count, 2 * half), 0)
    lane = iota((list_count, 2 * half), 1)
    for q_ref in q_refs:
        for p in range(q_ref.shape[0] // (2 * half)):
            ids = q_ref[p * 2 * half : (p + 1) * 2 * half, dim:].astype(F32).T
            owners, places = ids[:id_rows], ids[ids.shape[0] // 2 : ids.shape[0] // 2 + id_rows]
            places = jnp.where(owners == me.astype(F32), places, -1.0).astype(jnp.int32)
            probed = jnp.zeros(lists.shape, jnp.int32)
            for l in range(list_count):
                hit = jnp.where(places[: id_rows - 1] == l, 1, 0)
                probed = jnp.where(lists == l, jnp.max(hit, axis=0, keepdims=True), probed)
            probed = probed.astype(F32)
            appended = jnp.where(places[id_rows - 1 :] == lists, 1.0, 0.0)
            turned = [pltpu.roll(x, half, 1) for x in (probed, appended)]
            for i, block in enumerate(
                (jnp.where(lane < half, probed, turned[1]), jnp.where(lane < half, turned[0], appended))
            ):
                start = pl.multiple_of(src_ref[first] * list_count, list_count)
                marks_ref[pl.ds(start, list_count), :] = block
                first += 1


def rank_marks(list_count, marks, past=None):
    rows, width = marks.shape
    half = width // 2
    a, b = iota((width, width), 0), iota((width, width), 1)
    same = (a // half) == (b // half)
    earlier = jnp.where(same & (a < b), 1.0, 0.0).astype(BF16)
    every = jnp.where(same, 1.0, 0.0).astype(BF16)
    r, s = iota((rows, rows), 0), iota((rows, rows), 1)
    alike = r % list_count == s % list_count
    before = jnp.where(alike & (s < r), 1.0, 0.0).astype(BF16)

    def counts(x):
        return jnp.dot(x.astype(BF16), every, preferred_element_type=F32).astype(BF16)

    place = jnp.dot(marks.astype(BF16), earlier, preferred_element_type=F32)
    place = place + jnp.dot(before, counts(marks), preferred_element_type=F32)
    if past is not None:
        place = place + jnp.dot(
            jnp.where(alike, 1.0, 0.0).astype(BF16), counts(past), preferred_element_type=F32
        )
    return jnp.where(marks > 0.5, place, -1.0).astype(jnp.int32)


def pair_ranks(ranks_ref, src_ref, first, list_count, half, part):
    blocks = []
    for i in range(2):
        start = pl.multiple_of(src_ref[first + i] * list_count, list_count)
        block = ranks_ref[pl.ds(start, list_count), :]
        blocks.append(block if i == part else pltpu.roll(block, half, 1))
    lane = iota(blocks[0].shape, 1)
    return jnp.where(lane < half, blocks[0], blocks[1])


def group_into(list_count, per_list, first_piece, src_ref, ranks_ref, old, q_refs, out_ref, pick, pairs_ref, starts):
    half = ranks_ref.shape[1] // 2
    depth = pick.shape[1]
    dim = out_ref.shape[1]
    block = per_list // 2
    lists_a_step = pick.shape[0] // block
    pair_count = depth // (2 * half)
    lowest = highest = None
    for p in range(pair_count):
        ranks = pair_ranks(ranks_ref, src_ref, first_piece + 2 * p, list_count, half, 0)
        pairs_ref[p * list_count : (p + 1) * list_count, :] = ranks
        low = jnp.where(ranks < 0, per_list, ranks)
        lowest = low if p == 0 else jnp.minimum(lowest, low)
        highest = ranks if p == 0 else jnp.maximum(highest, ranks)
    firsts = []
    for l in range(list_count):
        if old:
            low = jnp.min(lowest[l : l + 1, :])
            firsts.append(jnp.minimum(low - low % 16, block))
        else:
            firsts.append(0)
        beyond = jnp.max(highest[l : l + 1, :]) >= firsts[l] + block
        starts[l] = firsts[l]
        starts[list_count + l] = beyond.astype(jnp.int32)
    place = iota((block, 2 * half), 0)

    def product(count):
        total = None
        at = 0
        for q_ref in q_refs:
            n = q_ref.shape[0]
            term = jnp.dot(pick[:count, at : at + n], q_ref[:, :dim], preferred_element_type=F32)
            total = term if total is None else total + term
            at += n
        return total.astype(BF16)

    for step in range(list_count // lists_a_step):
        for i in range(lists_a_step):
            l = step * lists_a_step + i
            for p in range(pair_count):
                ranks = pairs_ref[p * list_count + l : p * list_count + l + 1, :] - firsts[l]
                pick[i * block : (i + 1) * block, p * 2 * half : (p + 1) * 2 * half] = jnp.where(
                    ranks == place, 1.0, 0.0
                ).astype(BF16)
        total = product(pick.shape[0])
        for i in range(lists_a_step):
            l = step * lists_a_step + i
            rows = pl.ds(pl.multiple_of(l * per_list + firsts[l], 16), block)
            part = total[i * block : (i + 1) * block]
            out_ref[rows, :] = out_ref[rows, :] + part if old else part
            if not old:
                out_ref[l * per_list + block : (l + 1) * per_list, :] = jnp.zeros((per_list - block, dim), BF16)

    @pl.loop(0, list_count)
    def _(l):
        @pl.when(starts[list_count + l] > 0)
        def _():
            for p in range(pair_count):
                ranks = pairs_ref[pl.ds(p * list_count + l, 1), :]
                ranks = jnp.where(ranks >= starts[l] + block, ranks - block, -1)
                pick[:block, p * 2 * half : (p + 1) * 2 * half] = jnp.where(ranks == place, 1.0, 0.0).astype(BF16)
            rows = pl.ds(pl.multiple_of(l * per_list + block, 16), block)
            out_ref[rows, :] = out_ref[rows, :] + product(block)


def group_body(list_count, per_list, id_rows, src_ref, *refs):
    q_refs, (out_ref, marks_ref, ranks_ref, pick, pairs, starts) = refs[:-6], refs[-6:]
    unpack(q_refs, src_ref, 0, list_count, id_rows, out_ref.shape[1], marks_ref)
    ranks_ref[...] = rank_marks(list_count, marks_ref[...])
    group_into(list_count, per_list, 0, src_ref, ranks_ref, False, q_refs, out_ref, pick, pairs, starts)


def score_body(per_list, id_rows, first_piece, fill_ref, rows, src_ref, old_marks_ref, old_ranks_ref, _, *refs):
    q_refs, (out_ref, marks_ref, grouped_ref, ranks_ref, pick, best, pairs, starts) = refs[:-8], refs[-8:]
    list_count, _, dim = rows.shape
    senders, _, width = out_ref.shape
    unpack(q_refs, src_ref, first_piece, list_count, id_rows, dim, marks_ref)
    ranks_ref[...] = rank_marks(list_count, marks_ref[...], old_marks_ref[...])
    group_into(list_count, per_list, first_piece, src_ref, ranks_ref, True, q_refs, grouped_ref, pick, pairs, starts)
    for l in range(list_count):
        scores = lax.dot_general(
            rows[l],
            grouped_ref[l * per_list : (l + 1) * per_list, :],
            (((1,), (1,)), ((), ())),
            preferred_element_type=F32,
        )
        scores = jnp.where(iota(scores.shape, 0) < fill_ref[l], scores, -jnp.inf)
        best[l : l + 1, :] = jnp.max(scores, axis=0, keepdims=True)
    for s in range(senders):
        at = slice(s * list_count, (s + 1) * list_count)
        ranks = jnp.maximum(ranks_ref[at, :], old_ranks_ref[at, :])
        found = jnp.zeros(ranks.shape, F32)
        for c in range(per_list // width):
            index = jnp.clip(ranks - c * width, 0, width - 1)
            got = jnp.take_along_axis(best[:, c * width : (c + 1) * width], index, axis=1)
            found = jnp.where((ranks >= c * width) & (ranks < (c + 1) * width), got, found)
        out_ref[s] = found


def pick_body(got_ref, ids_ref, out_ref):
    probe_count = ids_ref.shape[0]
    lists = iota((got_ref.shape[0], ids_ref.shape[1]), 0)
    got = got_ref[:, : ids_ref.shape[1]]
    rows = []
    for j in range(probe_count):
        rows.append(jnp.sum(jnp.where(lists == ids_ref[j : j + 1, :], got, 0.0), axis=0, keepdims=True))
    out_ref[...] = jnp.concatenate(rows, axis=0)


def append_body(list_count, slots, src_ref, old_marks_ref, marks_ref, center_ref, sums_ref, *refs):
    q_refs, (codes_ref, scales_ref, sums_out_ref, ranks_ref, pick) = refs[:-5], refs[-5:]
    ranks_ref[...] = rank_marks(list_count, old_marks_ref[...] + marks_ref[...])
    half = ranks_ref.shape[1] // 2
    dim = center_ref.shape[1]
    place = iota((slots, 2 * half), 0)
    piece = 0
    total = jnp.zeros((list_count * slots, dim), F32)
    live = jnp.zeros((list_count * slots, 1), F32)
    for q_ref in q_refs:
        n = q_ref.shape[0]
        for p in range(n // (2 * half)):
            ranks = pair_ranks(ranks_ref, src_ref, piece, list_count, half, 1)
            piece += 2
            for l in range(list_count):
                hit = jnp.where(ranks[l : l + 1, :] == place, 1.0, 0.0)
                pick[l * slots : (l + 1) * slots, p * 2 * half : (p + 1) * 2 * half] = hit.astype(BF16)
        chosen = pick[:, :n]
        live = live + jnp.sum(chosen.astype(F32), axis=1, keepdims=True)
        total = total + jnp.dot(chosen, q_ref[:, :dim], preferred_element_type=F32)
    for l in range(list_count):
        rows = slice(l * slots, (l + 1) * slots)
        used = live[rows, :] > 0.5
        residual = jnp.where(used, total[rows, :] - center_ref[l : l + 1, :], 0.0)
        scale = jnp.max(jnp.abs(residual), axis=1, keepdims=True) + 1e-6
        codes_ref[l] = (residual / scale).astype(BF16)
        scales_ref[l : l + 1, :] = jnp.where(used, scale, 0.0).T
        sums_out_ref[l : l + 1, :] = sums_ref[l : l + 1, :] + jnp.sum(residual, axis=0, keepdims=True)


def swap_pairs(rows, cols, of):
    pairs = []
    for lr in range(rows):
        for lc in range(cols):
            to = of(lr, lc)
            pairs.append((lr * cols + lc, to[0] * cols + to[1]))
    return pairs


def after(x, *others):
    return lax.optimization_barrier((x, *others))[0]


def swap_core(x, rows, cols):
    return lax.ppermute(x, AXES, swap_pairs(rows, cols, lambda r, c: (r ^ 1, c)))


def gather_queries(queries, rows, cols, group_early):
    me = lax.axis_index(AXES)
    if (rows, cols) != (8, 4):
        whole = lax.all_gather(queries, AXES, axis=0, tiled=True)
        half = whole.shape[0] // 2
        sources = jnp.append(jnp.arange(rows * cols, dtype=jnp.int32), me)
        return [whole[:half]], [whole[half:]], sources, group_early(sources, [whole[:half]])

    def send(x, of):
        return lax.ppermute(x, AXES, swap_pairs(rows, cols, of))

    def first(x):
        return jnp.concatenate([x, send(x, lambda r, c: (r ^ (4 if r & 1 else 2), c))], 0)

    def second(x):
        return jnp.concatenate([x, send(x, lambda r, c: (r ^ (2 if r & 1 else 4), c))], 0)

    def other(x):
        return [x, swap_core(x, rows, cols)]

    r, c = lax.axis_index("lr"), lax.axis_index("lc")
    sources = []
    for planes in ((0, 1), (2, 3)):
        for core in (0, 1):
            odd = (r ^ core) & 1
            one, two = jnp.where(odd == 1, 4, 2), jnp.where(odd == 1, 2, 4)
            for hops in range(4):
                row = r ^ core
                row = row ^ one if hops & 1 else row
                row = row ^ two if hops & 2 else row
                sources += [row * cols + (c ^ plane) for plane in planes]
    sources = jnp.stack(sources + [me]).astype(jnp.int32)

    z1, z2, z3 = (send(queries, lambda r, c, k=k: (r, c ^ k)) for k in (1, 2, 3))
    pair = jnp.concatenate([queries, z1], 0)
    far = jnp.concatenate([z2, z3], 0)
    far = first(far)
    part = other(after(second(first(pair)), far))
    far = second(after(far, part[1]))
    grouped = group_early(sources, part)
    return part, other(after(far, *grouped)), sources, grouped


def local(queries, probes, assign, list_rows, list_fill, centroids, list_sums):
    rows, cols = lax.axis_size("lr"), lax.axis_size("lc")
    group = rows * cols
    list_count, row_count, dim = list_rows.shape
    query_count, probe_count = probes.shape
    pair_cap = 2 * query_count * probe_count // group
    append_cap = max(2, 2 * query_count // group)
    per_list = group * pair_cap // list_count
    slots = group * append_cap // list_count
    width = 2 * query_count
    total_lists = group * list_count

    ids = jnp.concatenate([probes, assign[:, None]], axis=1)
    id_rows = probe_count + 1
    id_lanes = 64
    spare = jnp.zeros((query_count, id_lanes - id_rows), jnp.int32)
    digits = jnp.concatenate([ids // list_count, spare, ids % list_count, spare], axis=1)
    packed = jnp.concatenate([queries, digits.astype(BF16)], axis=1)

    marks_shape = jax.ShapeDtypeStruct((total_lists, width), F32)
    ranks_shape = jax.ShapeDtypeStruct((total_lists, width), jnp.int32)

    def working(depth):
        return [
            pltpu.VMEM((2 * per_list, depth), BF16),
            pltpu.VMEM((depth // width * list_count, width), jnp.int32),
            pltpu.SMEM((2 * list_count,), jnp.int32),
        ]

    def group_early(sources, part):
        depth = sum(x.shape[0] for x in part)
        return call(
            functools.partial(group_body, list_count, per_list, id_rows),
            [jax.ShapeDtypeStruct((list_count * per_list, dim), BF16), marks_shape, ranks_shape],
            sources,
            *part,
            specs=[SMEM] + [VMEM] * len(part),
            scratch=working(depth),
            flops=2 * list_count * per_list * depth * dim,
            limit=28,
            name="group",
        )

    part, rest, sources, (grouped, old_marks, old_ranks) = gather_queries(packed, rows, cols, group_early)
    chunks = part + rest
    first = sum(x.shape[0] for x in part) // query_count
    depth = sum(x.shape[0] for x in rest)
    best, marks, _ = call(
        functools.partial(score_body, per_list, id_rows, first),
        [
            jax.ShapeDtypeStruct((group, list_count, width), F32),
            marks_shape,
            jax.ShapeDtypeStruct(grouped.shape, BF16),
        ],
        list_fill,
        list_rows,
        sources,
        old_marks,
        old_ranks,
        grouped,
        *rest,
        specs=[SMEM, VMEM, SMEM] + [VMEM] * (3 + len(rest)),
        scratch=[
            pltpu.VMEM((total_lists, width), jnp.int32),
            working(depth)[0],
            pltpu.VMEM((list_count, per_list), F32),
            *working(depth)[1:],
        ],
        alias={5: 2},
        limit=28,
        name="score",
    )
    got = lax.all_to_all(best, AXES, split_axis=0, concat_axis=0, tiled=True)
    dup_max = call(
        pick_body,
        jax.ShapeDtypeStruct((probe_count, query_count), F32),
        got.reshape(total_lists, width),
        probes.T,
        specs=[VMEM, VMEM],
        name="pick",
    )

    codes, scales, new_sums = call(
        functools.partial(append_body, list_count, slots),
        [
            jax.ShapeDtypeStruct((list_count, slots, dim), BF16),
            jax.ShapeDtypeStruct((list_count, slots), F32),
            jax.ShapeDtypeStruct((list_count, dim), F32),
        ],
        sources,
        old_marks,
        marks,
        centroids,
        list_sums,
        *chunks,
        specs=[SMEM] + [VMEM] * (4 + len(chunks)),
        scratch=[pltpu.VMEM((total_lists, width), jnp.int32), pltpu.VMEM((list_count * slots, max(x.shape[0] for x in chunks)), BF16)],
        name="append",
    )
    return dup_max.T, codes, scales, new_sums


def solution(mesh):
    split = P(AXES, None)
    return jax.shard_map(
        local,
        mesh=mesh,
        in_specs=(split, split, P(AXES), P(AXES, None, None), P(AXES), split, split),
        out_specs=(split, P(AXES, None, None), split, split),
        check_vma=False,
    )
```

```python
import functools

import jax
import jax.numpy as jnp
from jax import lax
from jax.experimental import pallas as pl
from jax.experimental.pallas import tpu as pltpu
from jax.sharding import PartitionSpec as P

AXES = ("lr", "lc")
VMEM = pl.BlockSpec(memory_space=pltpu.VMEM)
SMEM = pl.BlockSpec(memory_space=pltpu.SMEM)
BF16 = jnp.bfloat16
F32 = jnp.float32


def call(body, out_shape, *args, specs, name, scratch=(), flops=0, limit=24, alias=None):
    many = isinstance(out_shape, (list, tuple))
    return pl.pallas_call(
        body,
        in_specs=list(specs),
        out_specs=[VMEM] * len(out_shape) if many else VMEM,
        out_shape=out_shape,
        scratch_shapes=list(scratch),
        input_output_aliases=alias or {},
        compiler_params=pltpu.CompilerParams(vmem_limit_bytes=limit * 2**20),
        cost_estimate=pl.CostEstimate(flops=flops, bytes_accessed=0, transcendentals=0),
        name=name,
    )(*args)


def iota(shape, dim):
    return lax.broadcasted_iota(jnp.int32, shape, dim)


def over(x, n):
    if n & (n - 1):
        return x // n, x % n
    return x >> (n.bit_length() - 1), x & (n - 1)


def unpack(q_refs, src_ref, first, list_count, id_rows, dim, marks_ref):
    half = marks_ref.shape[1] // 2
    me = src_ref[src_ref.shape[0] - 1]
    marks_ref[...] = jnp.zeros(marks_ref.shape, F32)
    lists = iota((list_count, 2 * half), 0)
    lane = iota((list_count, 2 * half), 1)
    for q_ref in q_refs:
        for p in range(q_ref.shape[0] // (2 * half)):
            ids = q_ref[p * 2 * half : (p + 1) * 2 * half, dim:].astype(F32).T
            owners, places = ids[:id_rows], ids[ids.shape[0] // 2 : ids.shape[0] // 2 + id_rows]
            places = jnp.where(owners == me.astype(F32), places, -1.0).astype(jnp.int32)
            probed = jnp.zeros(lists.shape, jnp.int32)
            for l in range(list_count):
                hit = jnp.where(places[: id_rows - 1] == l, 1, 0)
                probed = jnp.where(lists == l, jnp.max(hit, axis=0, keepdims=True), probed)
            probed = probed.astype(F32)
            appended = jnp.where(places[id_rows - 1 :] == lists, 1.0, 0.0)
            turned = [pltpu.roll(x, half, 1) for x in (probed, appended)]
            for i, block in enumerate(
                (jnp.where(lane < half, probed, turned[1]), jnp.where(lane < half, turned[0], appended))
            ):
                start = pl.multiple_of(src_ref[first] * list_count, list_count)
                marks_ref[pl.ds(start, list_count), :] = block
                first += 1


def rank_marks(list_count, marks, past=None):
    rows, width = marks.shape
    half = width // 2
    a, b = iota((width, width), 0), iota((width, width), 1)
    same = over(a, half)[0] == over(b, half)[0]
    earlier = jnp.where(same & (a < b), 1.0, 0.0).astype(BF16)
    every = jnp.where(same, 1.0, 0.0).astype(BF16)
    r, s = iota((rows, rows), 0), iota((rows, rows), 1)
    alike = over(r, list_count)[1] == over(s, list_count)[1]
    before = jnp.where(alike & (s < r), 1.0, 0.0).astype(BF16)

    def counts(x):
        return jnp.dot(x.astype(BF16), every, preferred_element_type=F32).astype(BF16)

    place = jnp.dot(marks.astype(BF16), earlier, preferred_element_type=F32)
    place = place + jnp.dot(before, counts(marks), preferred_element_type=F32)
    if past is not None:
        place = place + jnp.dot(
            jnp.where(alike, 1.0, 0.0).astype(BF16), counts(past), preferred_element_type=F32
        )
    return jnp.where(marks > 0.5, place, -1.0).astype(jnp.int32)


def pair_ranks(ranks_ref, src_ref, first, list_count, half, part):
    blocks = []
    for i in range(2):
        start = pl.multiple_of(src_ref[first + i] * list_count, list_count)
        block = ranks_ref[pl.ds(start, list_count), :]
        blocks.append(block if i == part else pltpu.roll(block, half, 1))
    lane = iota(blocks[0].shape, 1)
    return jnp.where(lane < half, blocks[0], blocks[1])


def group_into(list_count, per_list, first_piece, src_ref, ranks_ref, old, q_refs, out_ref, pick, pairs_ref, starts):
    half = ranks_ref.shape[1] // 2
    depth = pick.shape[1]
    dim = out_ref.shape[1]
    block = per_list // 2
    lists_a_step = pick.shape[0] // block
    pair_count = depth // (2 * half)
    lowest = highest = None
    for p in range(pair_count):
        ranks = pair_ranks(ranks_ref, src_ref, first_piece + 2 * p, list_count, half, 0)
        pairs_ref[p * list_count : (p + 1) * list_count, :] = ranks
        low = jnp.where(ranks < 0, per_list, ranks)
        lowest = low if p == 0 else jnp.minimum(lowest, low)
        highest = ranks if p == 0 else jnp.maximum(highest, ranks)
    low = jnp.min(lowest, axis=1, keepdims=True)
    low = jnp.minimum(low - (low & 15), block) if old else jnp.zeros_like(low)
    beyond = (jnp.max(highest, axis=1, keepdims=True) >= low + block).astype(jnp.int32)
    firsts = []
    for l in range(list_count):
        firsts.append(low[l, 0] if old else 0)
        starts[l] = firsts[l]
        starts[list_count + l] = beyond[l, 0]
    place = iota((block, 2 * half), 0).astype(BF16)
    one, none = jnp.ones(place.shape, BF16), jnp.zeros(place.shape, BF16)

    def product(count):
        total = None
        at = 0
        for q_ref in q_refs:
            n = q_ref.shape[0]
            term = jnp.dot(pick[:count, at : at + n], q_ref[:, :dim], preferred_element_type=F32)
            total = term if total is None else total + term
            at += n
        return total.astype(BF16)

    for step in range(list_count // lists_a_step):
        for i in range(lists_a_step):
            l = step * lists_a_step + i
            for p in range(pair_count):
                ranks = pairs_ref[p * list_count + l : p * list_count + l + 1, :] - firsts[l]
                pick[i * block : (i + 1) * block, p * 2 * half : (p + 1) * 2 * half] = jnp.where(
                    ranks.astype(F32).astype(BF16) == place, one, none
                )
        total = product(pick.shape[0])
        for i in range(lists_a_step):
            l = step * lists_a_step + i
            rows = pl.ds(pl.multiple_of(l * per_list + firsts[l], 16), block)
            part = total[i * block : (i + 1) * block]
            out_ref[rows, :] = out_ref[rows, :] + part if old else part
            if not old:
                out_ref[l * per_list + block : (l + 1) * per_list, :] = jnp.zeros((per_list - block, dim), BF16)

    @pl.loop(0, list_count)
    def _(l):
        @pl.when(starts[list_count + l] > 0)
        def _():
            for p in range(pair_count):
                ranks = pairs_ref[pl.ds(p * list_count + l, 1), :]
                ranks = jnp.where(ranks >= starts[l] + block, ranks - block, -1)
                pick[:block, p * 2 * half : (p + 1) * 2 * half] = jnp.where(
                    ranks.astype(F32).astype(BF16) == place, one, none
                )
            rows = pl.ds(pl.multiple_of(l * per_list + block, 16), block)
            out_ref[rows, :] = out_ref[rows, :] + product(block)


def group_body(list_count, per_list, id_rows, first_piece, src_ref, *refs):
    old, q_refs = (refs[:3], refs[3:-6]) if first_piece else (None, refs[:-6])
    out_ref, marks_ref, ranks_ref, pick, pairs, starts = refs[-6:]
    unpack(q_refs, src_ref, first_piece, list_count, id_rows, out_ref.shape[1], marks_ref)
    ranks_ref[...] = rank_marks(list_count, marks_ref[...], old[1][...] if old else None)
    group_into(
        list_count, per_list, first_piece, src_ref, ranks_ref, bool(old), q_refs, out_ref, pick, pairs, starts
    )
    if old:
        marks_ref[...] = marks_ref[...] + old[1][...]
        ranks_ref[...] = jnp.maximum(ranks_ref[...], old[2][...])


def score_body(per_list, id_rows, first_piece, fill_ref, rows, src_ref, old_marks_ref, old_ranks_ref, _, *refs):
    q_refs, (out_ref, marks_ref, grouped_ref, ranks_ref, pick, best, pairs, starts) = refs[:-8], refs[-8:]
    list_count, _, dim = rows.shape
    senders, _, width = out_ref.shape
    unpack(q_refs, src_ref, first_piece, list_count, id_rows, dim, marks_ref)
    ranks_ref[...] = rank_marks(list_count, marks_ref[...], old_marks_ref[...])
    group_into(list_count, per_list, first_piece, src_ref, ranks_ref, True, q_refs, grouped_ref, pick, pairs, starts)
    for l in range(list_count):
        scores = lax.dot_general(
            rows[l],
            grouped_ref[l * per_list : (l + 1) * per_list, :],
            (((1,), (1,)), ((), ())),
            preferred_element_type=F32,
        )
        scores = jnp.where(iota(scores.shape, 0) < fill_ref[l], scores, -jnp.inf)
        best[l : l + 1, :] = jnp.max(scores, axis=0, keepdims=True)
    for s in range(senders):
        at = slice(s * list_count, (s + 1) * list_count)
        ranks = jnp.maximum(ranks_ref[at, :], old_ranks_ref[at, :])
        found = jnp.zeros(ranks.shape, F32)
        for c in range(per_list // width):
            index = jnp.clip(ranks - c * width, 0, width - 1)
            got = jnp.take_along_axis(best[:, c * width : (c + 1) * width], index, axis=1)
            found = jnp.where((ranks >= c * width) & (ranks < (c + 1) * width), got, found)
        out_ref[s] = found


def pick_body(got_ref, ids_ref, out_ref):
    probe_count = ids_ref.shape[0]
    lists = iota((got_ref.shape[0], ids_ref.shape[1]), 0)
    got = got_ref[:, : ids_ref.shape[1]]
    rows = []
    for j in range(probe_count):
        rows.append(jnp.sum(jnp.where(lists == ids_ref[j : j + 1, :], got, 0.0), axis=0, keepdims=True))
    out_ref[...] = jnp.concatenate(rows, axis=0)


def append_body(list_count, slots, src_ref, old_marks_ref, marks_ref, center_ref, sums_ref, *refs):
    q_refs, (codes_ref, scales_ref, sums_out_ref, ranks_ref, pick) = refs[:-5], refs[-5:]
    ranks_ref[...] = rank_marks(list_count, old_marks_ref[...] + marks_ref[...])
    half = ranks_ref.shape[1] // 2
    dim = center_ref.shape[1]
    place = iota((slots, 2 * half), 0)
    piece = 0
    total = jnp.zeros((list_count * slots, dim), F32)
    live = jnp.zeros((list_count * slots, 1), F32)
    for q_ref in q_refs:
        n = q_ref.shape[0]
        for p in range(n // (2 * half)):
            ranks = pair_ranks(ranks_ref, src_ref, piece, list_count, half, 1)
            piece += 2
            for l in range(list_count):
                hit = jnp.where(ranks[l : l + 1, :] == place, 1.0, 0.0)
                pick[l * slots : (l + 1) * slots, p * 2 * half : (p + 1) * 2 * half] = hit.astype(BF16)
        chosen = pick[:, :n]
        live = live + jnp.sum(chosen.astype(F32), axis=1, keepdims=True)
        total = total + jnp.dot(chosen, q_ref[:, :dim], preferred_element_type=F32)
    for l in range(list_count):
        rows = slice(l * slots, (l + 1) * slots)
        used = live[rows, :] > 0.5
        residual = jnp.where(used, total[rows, :] - center_ref[l : l + 1, :], 0.0)
        scale = jnp.max(jnp.abs(residual), axis=1, keepdims=True) + 1e-6
        codes_ref[l] = (residual / scale).astype(BF16)
        scales_ref[l : l + 1, :] = jnp.where(used, scale, 0.0).T
        sums_out_ref[l : l + 1, :] = sums_ref[l : l + 1, :] + jnp.sum(residual, axis=0, keepdims=True)


def swap_pairs(rows, cols, of):
    pairs = []
    for lr in range(rows):
        for lc in range(cols):
            to = of(lr, lc)
            pairs.append((lr * cols + lc, to[0] * cols + to[1]))
    return pairs


def after(x, *others):
    return lax.optimization_barrier((x, *others))[0]


def swap_core(x, rows, cols):
    return lax.ppermute(x, AXES, swap_pairs(rows, cols, lambda r, c: (r ^ 1, c)))


def gather_queries(queries, rows, cols, group_early):
    me = lax.axis_index(AXES)
    if (rows, cols) != (8, 4):
        whole = lax.all_gather(queries, AXES, axis=0, tiled=True)
        half = whole.shape[0] // 2
        sources = jnp.append(jnp.arange(rows * cols, dtype=jnp.int32), me)
        return [whole[:half]], [whole[half:]], sources, group_early(sources, [whole[:half]])

    def send(x, of):
        return lax.ppermute(x, AXES, swap_pairs(rows, cols, of))

    def first(x):
        return jnp.concatenate([x, send(x, lambda r, c: (r ^ (4 if r & 1 else 2), c))], 0)

    def second(x):
        return jnp.concatenate([x, send(x, lambda r, c: (r ^ (2 if r & 1 else 4), c))], 0)

    def other(x):
        return [x, swap_core(x, rows, cols)]

    r, c = lax.axis_index("lr"), lax.axis_index("lc")
    sources = []
    for planes in ((0, 1), (2, 3)):
        for core in (0, 1):
            odd = (r ^ core) & 1
            one, two = jnp.where(odd == 1, 4, 2), jnp.where(odd == 1, 2, 4)
            for hops in range(4):
                row = r ^ core
                row = row ^ one if hops & 1 else row
                row = row ^ two if hops & 2 else row
                sources += [row * cols + (c ^ plane) for plane in planes]
    sources = jnp.stack(sources + [me]).astype(jnp.int32)

    z1, z2, z3 = (send(queries, lambda r, c, k=k: (r, c ^ k)) for k in (1, 2, 3))
    pair = jnp.concatenate([queries, z1], 0)
    far = jnp.concatenate([z2, z3], 0)
    near = second(first(pair))
    far = second(first(far))
    pieces = near.shape[0] // queries.shape[0]
    half = group_early(sources, [near])
    part = other(after(near, *half))
    part[0] = near
    grouped = group_early(sources, part[1:], pieces, tuple(half))
    return part, other(far), sources, grouped


def local(queries, probes, assign, list_rows, list_fill, centroids, list_sums):
    rows, cols = lax.axis_size("lr"), lax.axis_size("lc")
    group = rows * cols
    list_count, row_count, dim = list_rows.shape
    query_count, probe_count = probes.shape
    pair_cap = 2 * query_count * probe_count // group
    append_cap = max(2, 2 * query_count // group)
    per_list = group * pair_cap // list_count
    slots = group * append_cap // list_count
    width = 2 * query_count
    total_lists = group * list_count

    ids = jnp.concatenate([probes, assign[:, None]], axis=1)
    id_rows = probe_count + 1
    id_lanes = 64
    spare = jnp.zeros((query_count, id_lanes - id_rows), jnp.int32)
    digits = jnp.concatenate([ids // list_count, spare, ids % list_count, spare], axis=1)
    packed = jnp.concatenate([queries, digits.astype(BF16)], axis=1)

    marks_shape = jax.ShapeDtypeStruct((total_lists, width), F32)
    ranks_shape = jax.ShapeDtypeStruct((total_lists, width), jnp.int32)

    def working(depth):
        return [
            pltpu.VMEM((2 * per_list, depth), BF16),
            pltpu.VMEM((depth // width * list_count, width), jnp.int32),
            pltpu.SMEM((2 * list_count,), jnp.int32),
        ]

    def group_early(sources, part, first=0, old=()):
        depth = sum(x.shape[0] for x in part)
        return call(
            functools.partial(group_body, list_count, per_list, id_rows, first),
            [jax.ShapeDtypeStruct((list_count * per_list, dim), BF16), marks_shape, ranks_shape],
            sources,
            *old,
            *part,
            specs=[SMEM] + [VMEM] * (len(old) + len(part)),
            scratch=working(depth),
            flops=2 * list_count * per_list * depth * dim,
            limit=28,
            alias={1: 0} if old else None,
            name="group",
        )

    part, rest, sources, (grouped, old_marks, old_ranks) = gather_queries(packed, rows, cols, group_early)
    chunks = part + rest
    first = sum(x.shape[0] for x in part) // query_count
    depth = sum(x.shape[0] for x in rest)
    best, marks, _ = call(
        functools.partial(score_body, per_list, id_rows, first),
        [
            jax.ShapeDtypeStruct((group, list_count, width), F32),
            marks_shape,
            jax.ShapeDtypeStruct(grouped.shape, BF16),
        ],
        list_fill,
        list_rows,
        sources,
        old_marks,
        old_ranks,
        grouped,
        *rest,
        specs=[SMEM, VMEM, SMEM] + [VMEM] * (3 + len(rest)),
        scratch=[
            pltpu.VMEM((total_lists, width), jnp.int32),
            working(depth)[0],
            pltpu.VMEM((list_count, per_list), F32),
            *working(depth)[1:],
        ],
        alias={5: 2},
        limit=28,
        name="score",
    )
    got = lax.all_to_all(best, AXES, split_axis=0, concat_axis=0, tiled=True)
    dup_max = call(
        pick_body,
        jax.ShapeDtypeStruct((probe_count, query_count), F32),
        got.reshape(total_lists, width),
        probes.T,
        specs=[VMEM, VMEM],
        name="pick",
    )

    codes, scales, new_sums = call(
        functools.partial(append_body, list_count, slots),
        [
            jax.ShapeDtypeStruct((list_count, slots, dim), BF16),
            jax.ShapeDtypeStruct((list_count, slots), F32),
            jax.ShapeDtypeStruct((list_count, dim), F32),
        ],
        sources,
        old_marks,
        marks,
        centroids,
        list_sums,
        *chunks,
        specs=[SMEM] + [VMEM] * (4 + len(chunks)),
        scratch=[pltpu.VMEM((total_lists, width), jnp.int32), pltpu.VMEM((list_count * slots, max(x.shape[0] for x in chunks)), BF16)],
        name="append",
    )
    return dup_max.T, codes, scales, new_sums


def solution(mesh):
    split = P(AXES, None)
    return jax.shard_map(
        local,
        mesh=mesh,
        in_specs=(split, split, P(AXES), P(AXES, None, None), P(AXES), split, split),
        out_specs=(split, P(AXES, None, None), split, split),
        check_vma=False,
    )
```

```python
import functools

import jax
import jax.numpy as jnp
from jax import lax
from jax.experimental import pallas as pl
from jax.experimental.pallas import tpu as pltpu
from jax.sharding import PartitionSpec as P

AXES = ("lr", "lc")
VMEM = pl.BlockSpec(memory_space=pltpu.VMEM)
SMEM = pl.BlockSpec(memory_space=pltpu.SMEM)
BF16 = jnp.bfloat16
F32 = jnp.float32


def call(body, out_shape, *args, specs, name, scratch=(), flops=0, limit=24, alias=None):
    many = isinstance(out_shape, (list, tuple))
    return pl.pallas_call(
        body,
        in_specs=list(specs),
        out_specs=[VMEM] * len(out_shape) if many else VMEM,
        out_shape=out_shape,
        scratch_shapes=list(scratch),
        input_output_aliases=alias or {},
        compiler_params=pltpu.CompilerParams(vmem_limit_bytes=limit * 2**20),
        cost_estimate=pl.CostEstimate(flops=flops, bytes_accessed=0, transcendentals=0),
        name=name,
    )(*args)


def iota(shape, dim):
    return lax.broadcasted_iota(jnp.int32, shape, dim)


def over(x, n):
    if n & (n - 1):
        return x // n, x % n
    return x >> (n.bit_length() - 1), x & (n - 1)


def unpack(q_refs, src_ref, first, list_count, id_rows, dim, marks_ref):
    half = marks_ref.shape[1] // 2
    me = src_ref[src_ref.shape[0] - 1]
    marks_ref[...] = jnp.zeros(marks_ref.shape, F32)
    lists = iota((list_count, 2 * half), 0)
    lane = iota((list_count, 2 * half), 1)
    for q_ref in q_refs:
        for p in range(q_ref.shape[0] // (2 * half)):
            ids = q_ref[p * 2 * half : (p + 1) * 2 * half, dim:].astype(F32).T
            owners, places = ids[:id_rows], ids[ids.shape[0] // 2 : ids.shape[0] // 2 + id_rows]
            places = jnp.where(owners == me.astype(F32), places, -1.0).astype(jnp.int32)
            probed = jnp.zeros(lists.shape, jnp.int32)
            for l in range(list_count):
                hit = jnp.where(places[: id_rows - 1] == l, 1, 0)
                probed = jnp.where(lists == l, jnp.max(hit, axis=0, keepdims=True), probed)
            probed = probed.astype(F32)
            appended = jnp.where(places[id_rows - 1 :] == lists, 1.0, 0.0)
            turned = [pltpu.roll(x, half, 1) for x in (probed, appended)]
            for i, block in enumerate(
                (jnp.where(lane < half, probed, turned[1]), jnp.where(lane < half, turned[0], appended))
            ):
                start = pl.multiple_of(src_ref[first] * list_count, list_count)
                marks_ref[pl.ds(start, list_count), :] = block
                first += 1


def rank_marks(list_count, marks, past=None):
    rows, width = marks.shape
    half = width // 2
    a, b = iota((width, width), 0), iota((width, width), 1)
    same = over(a, half)[0] == over(b, half)[0]
    earlier = jnp.where(same & (a < b), 1.0, 0.0).astype(BF16)
    every = jnp.where(same, 1.0, 0.0).astype(BF16)
    r, s = iota((rows, rows), 0), iota((rows, rows), 1)
    alike = over(r, list_count)[1] == over(s, list_count)[1]
    before = jnp.where(alike & (s < r), 1.0, 0.0).astype(BF16)

    def counts(x):
        return jnp.dot(x.astype(BF16), every, preferred_element_type=F32).astype(BF16)

    place = jnp.dot(marks.astype(BF16), earlier, preferred_element_type=F32)
    place = place + jnp.dot(before, counts(marks), preferred_element_type=F32)
    if past is not None:
        place = place + jnp.dot(
            jnp.where(alike, 1.0, 0.0).astype(BF16), counts(past), preferred_element_type=F32
        )
    return jnp.where(marks > 0.5, place, -1.0).astype(jnp.int32)


def pair_ranks(ranks_ref, src_ref, first, list_count, half, part):
    blocks = []
    for i in range(2):
        start = pl.multiple_of(src_ref[first + i] * list_count, list_count)
        block = ranks_ref[pl.ds(start, list_count), :]
        blocks.append(block if i == part else pltpu.roll(block, half, 1))
    lane = iota(blocks[0].shape, 1)
    return jnp.where(lane < half, blocks[0], blocks[1])


def group_into(list_count, per_list, first_piece, src_ref, ranks_ref, old, q_refs, out_ref, pick, pairs_ref, starts):
    half = ranks_ref.shape[1] // 2
    depth = pick.shape[1]
    dim = out_ref.shape[1]
    block = per_list // 2
    lists_a_step = pick.shape[0] // block
    pair_count = depth // (2 * half)
    lowest = highest = None
    for p in range(pair_count):
        ranks = pair_ranks(ranks_ref, src_ref, first_piece + 2 * p, list_count, half, 0)
        pairs_ref[p * list_count : (p + 1) * list_count, :] = ranks
        low = jnp.where(ranks < 0, per_list, ranks)
        lowest = low if p == 0 else jnp.minimum(lowest, low)
        highest = ranks if p == 0 else jnp.maximum(highest, ranks)
    low = jnp.min(lowest, axis=1, keepdims=True)
    low = jnp.minimum(low - (low & 15), block) if old else jnp.zeros_like(low)
    beyond = (jnp.max(highest, axis=1, keepdims=True) >= low + block).astype(jnp.int32)
    firsts = []
    for l in range(list_count):
        firsts.append(low[l, 0] if old else 0)
        starts[l] = firsts[l]
        starts[list_count + l] = beyond[l, 0]
    place = iota((block, 2 * half), 0).astype(BF16)
    one, none = jnp.ones(place.shape, BF16), jnp.zeros(place.shape, BF16)

    def product(count):
        total = None
        at = 0
        for q_ref in q_refs:
            n = q_ref.shape[0]
            term = jnp.dot(pick[:count, at : at + n], q_ref[:, :dim], preferred_element_type=F32)
            total = term if total is None else total + term
            at += n
        return total.astype(BF16)

    for step in range(list_count // lists_a_step):
        for i in range(lists_a_step):
            l = step * lists_a_step + i
            for p in range(pair_count):
                ranks = pairs_ref[p * list_count + l : p * list_count + l + 1, :] - firsts[l]
                pick[i * block : (i + 1) * block, p * 2 * half : (p + 1) * 2 * half] = jnp.where(
                    ranks.astype(F32).astype(BF16) == place, one, none
                )
        total = product(pick.shape[0])
        for i in range(lists_a_step):
            l = step * lists_a_step + i
            rows = pl.ds(pl.multiple_of(l * per_list + firsts[l], 16), block)
            part = total[i * block : (i + 1) * block]
            out_ref[rows, :] = out_ref[rows, :] + part if old else part
            if not old:
                out_ref[l * per_list + block : (l + 1) * per_list, :] = jnp.zeros((per_list - block, dim), BF16)

    @pl.loop(0, list_count)
    def _(l):
        @pl.when(starts[list_count + l] > 0)
        def _():
            for p in range(pair_count):
                ranks = pairs_ref[pl.ds(p * list_count + l, 1), :]
                ranks = jnp.where(ranks >= starts[l] + block, ranks - block, -1)
                pick[:block, p * 2 * half : (p + 1) * 2 * half] = jnp.where(
                    ranks.astype(F32).astype(BF16) == place, one, none
                )
            rows = pl.ds(pl.multiple_of(l * per_list + block, 16), block)
            out_ref[rows, :] = out_ref[rows, :] + product(block)


def group_body(list_count, per_list, id_rows, first_piece, src_ref, *refs):
    old, q_refs = (refs[:3], refs[3:-6]) if first_piece else (None, refs[:-6])
    out_ref, marks_ref, ranks_ref, pick, pairs, starts = refs[-6:]
    unpack(q_refs, src_ref, first_piece, list_count, id_rows, out_ref.shape[1], marks_ref)
    ranks_ref[...] = rank_marks(list_count, marks_ref[...], old[1][...] if old else None)
    group_into(
        list_count, per_list, first_piece, src_ref, ranks_ref, bool(old), q_refs, out_ref, pick, pairs, starts
    )
    if old:
        marks_ref[...] = marks_ref[...] + old[1][...]
        ranks_ref[...] = jnp.maximum(ranks_ref[...], old[2][...])


def score_body(per_list, id_rows, first_piece, fill_ref, rows, src_ref, old_marks_ref, old_ranks_ref, _, *refs):
    q_refs, (out_ref, marks_ref, grouped_ref, ranks_ref, pick, best, pairs, starts) = refs[:-8], refs[-8:]
    list_count, _, dim = rows.shape
    width = out_ref.shape[1]
    senders = ranks_ref.shape[0] // list_count
    unpack(q_refs, src_ref, first_piece, list_count, id_rows, dim, marks_ref)
    ranks_ref[...] = rank_marks(list_count, marks_ref[...], old_marks_ref[...])
    group_into(list_count, per_list, first_piece, src_ref, ranks_ref, True, q_refs, grouped_ref, pick, pairs, starts)
    for l in range(list_count):
        scores = lax.dot_general(
            rows[l],
            grouped_ref[l * per_list : (l + 1) * per_list, :],
            (((1,), (1,)), ((), ())),
            preferred_element_type=F32,
        )
        scores = jnp.where(iota(scores.shape, 0) < fill_ref[l], scores, -jnp.inf)
        best[l : l + 1, :] = jnp.max(scores, axis=0, keepdims=True)
    for s in range(senders):
        at = slice(s * list_count, (s + 1) * list_count)
        ranks = jnp.maximum(ranks_ref[at, :], old_ranks_ref[at, :])
        found = jnp.zeros(ranks.shape, F32)
        for c in range(per_list // width):
            index = jnp.clip(ranks - c * width, 0, width - 1)
            got = jnp.take_along_axis(best[:, c * width : (c + 1) * width], index, axis=1)
            found = jnp.where((ranks >= c * width) & (ranks < (c + 1) * width), got, found)
        lane = iota((list_count // 2, width), 1)
        turned = pltpu.roll(found, width // 2, 1)
        packed = jnp.where(lane < width // 2, found[: list_count // 2], turned[list_count // 2 :])
        out_ref[s * (list_count // 2) : (s + 1) * (list_count // 2), :] = packed


def pick_body(list_count, got_ref, ids_ref, out_ref):
    probe_count, count = ids_ref.shape
    half = list_count // 2
    owner, place = over(ids_ref[...], list_count)
    second = jnp.where(place >= half, 1, 0)
    row = owner * half + place - second * half
    rows = iota(got_ref.shape, 0)
    row = jnp.concatenate([jnp.where(second == 0, row, -1), jnp.where(second == 1, row, -1)], axis=1)
    got = got_ref[...]
    found = []
    for j in range(probe_count):
        found.append(jnp.sum(jnp.where(rows == row[j : j + 1, :], got, 0.0), axis=0, keepdims=True))
    found = jnp.concatenate(found, axis=0)
    out_ref[...] = found[:, :count] + found[:, count:]


def append_body(list_count, slots, src_ref, old_marks_ref, marks_ref, center_ref, sums_ref, *refs):
    q_refs, (codes_ref, scales_ref, sums_out_ref, ranks_ref, pick) = refs[:-5], refs[-5:]
    ranks_ref[...] = rank_marks(list_count, old_marks_ref[...] + marks_ref[...])
    half = ranks_ref.shape[1] // 2
    dim = center_ref.shape[1]
    place = iota((slots, 2 * half), 0)
    piece = 0
    total = jnp.zeros((list_count * slots, dim), F32)
    live = jnp.zeros((list_count * slots, 1), F32)
    for q_ref in q_refs:
        n = q_ref.shape[0]
        for p in range(n // (2 * half)):
            ranks = pair_ranks(ranks_ref, src_ref, piece, list_count, half, 1)
            piece += 2
            for l in range(list_count):
                hit = jnp.where(ranks[l : l + 1, :] == place, 1.0, 0.0)
                pick[l * slots : (l + 1) * slots, p * 2 * half : (p + 1) * 2 * half] = hit.astype(BF16)
        chosen = pick[:, :n]
        live = live + jnp.sum(chosen.astype(F32), axis=1, keepdims=True)
        total = total + jnp.dot(chosen, q_ref[:, :dim], preferred_element_type=F32)
    for l in range(list_count):
        rows = slice(l * slots, (l + 1) * slots)
        used = live[rows, :] > 0.5
        residual = jnp.where(used, total[rows, :] - center_ref[l : l + 1, :], 0.0)
        scale = jnp.max(jnp.abs(residual), axis=1, keepdims=True) + 1e-6
        codes_ref[l] = (residual / scale).astype(BF16)
        scales_ref[l : l + 1, :] = jnp.where(used, scale, 0.0).T
        sums_out_ref[l : l + 1, :] = sums_ref[l : l + 1, :] + jnp.sum(residual, axis=0, keepdims=True)


def swap_pairs(rows, cols, of):
    pairs = []
    for lr in range(rows):
        for lc in range(cols):
            to = of(lr, lc)
            pairs.append((lr * cols + lc, to[0] * cols + to[1]))
    return pairs


def after(x, *others):
    return lax.optimization_barrier((x, *others))[0]


def swap_core(x, rows, cols):
    return lax.ppermute(x, AXES, swap_pairs(rows, cols, lambda r, c: (r ^ 1, c)))


def gather_queries(queries, rows, cols, group_early):
    me = lax.axis_index(AXES)
    if (rows, cols) != (8, 4):
        whole = lax.all_gather(queries, AXES, axis=0, tiled=True)
        half = whole.shape[0] // 2
        sources = jnp.append(jnp.arange(rows * cols, dtype=jnp.int32), me)
        return [whole[:half]], [whole[half:]], sources, group_early(sources, [whole[:half]])

    def send(x, of):
        return lax.ppermute(x, AXES, swap_pairs(rows, cols, of))

    def first(x):
        return jnp.concatenate([x, send(x, lambda r, c: (r ^ (4 if r & 1 else 2), c))], 0)

    def second(x):
        return jnp.concatenate([x, send(x, lambda r, c: (r ^ (2 if r & 1 else 4), c))], 0)

    def other(x):
        return [x, swap_core(x, rows, cols)]

    r, c = lax.axis_index("lr"), lax.axis_index("lc")
    sources = []
    for planes in ((0, 1), (2, 3)):
        for core in (0, 1):
            odd = (r ^ core) & 1
            one, two = jnp.where(odd == 1, 4, 2), jnp.where(odd == 1, 2, 4)
            for hops in range(4):
                row = r ^ core
                row = row ^ one if hops & 1 else row
                row = row ^ two if hops & 2 else row
                sources += [row * cols + (c ^ plane) for plane in planes]
    sources = jnp.stack(sources + [me]).astype(jnp.int32)

    z1, z2, z3 = (send(queries, lambda r, c, k=k: (r, c ^ k)) for k in (1, 2, 3))
    pair = jnp.concatenate([queries, z1], 0)
    far = jnp.concatenate([z2, z3], 0)
    near = second(first(pair))
    far = second(first(far))
    pieces = near.shape[0] // queries.shape[0]
    half = group_early(sources, [near])
    part = other(after(near, *half))
    part[0] = near
    grouped = group_early(sources, part[1:], pieces, tuple(half))
    return part, other(far), sources, grouped


def local(queries, probes, assign, list_rows, list_fill, centroids, list_sums):
    rows, cols = lax.axis_size("lr"), lax.axis_size("lc")
    group = rows * cols
    list_count, row_count, dim = list_rows.shape
    query_count, probe_count = probes.shape
    pair_cap = 2 * query_count * probe_count // group
    append_cap = max(2, 2 * query_count // group)
    per_list = group * pair_cap // list_count
    slots = group * append_cap // list_count
    width = 2 * query_count
    total_lists = group * list_count

    ids = jnp.concatenate([probes, assign[:, None]], axis=1)
    id_rows = probe_count + 1
    id_lanes = 64
    spare = jnp.zeros((query_count, id_lanes - id_rows), jnp.int32)
    digits = jnp.concatenate([ids // list_count, spare, ids % list_count, spare], axis=1)
    packed = jnp.concatenate([queries, digits.astype(BF16)], axis=1)

    marks_shape = jax.ShapeDtypeStruct((total_lists, width), F32)
    ranks_shape = jax.ShapeDtypeStruct((total_lists, width), jnp.int32)

    def working(depth):
        return [
            pltpu.VMEM((2 * per_list, depth), BF16),
            pltpu.VMEM((depth // width * list_count, width), jnp.int32),
            pltpu.SMEM((2 * list_count,), jnp.int32),
        ]

    def group_early(sources, part, first=0, old=()):
        depth = sum(x.shape[0] for x in part)
        return call(
            functools.partial(group_body, list_count, per_list, id_rows, first),
            [jax.ShapeDtypeStruct((list_count * per_list, dim), BF16), marks_shape, ranks_shape],
            sources,
            *old,
            *part,
            specs=[SMEM] + [VMEM] * (len(old) + len(part)),
            scratch=working(depth),
            flops=2 * list_count * per_list * depth * dim,
            limit=28,
            alias={1: 0} if old else None,
            name="group",
        )

    part, rest, sources, (grouped, old_marks, old_ranks) = gather_queries(packed, rows, cols, group_early)
    chunks = part + rest
    first = sum(x.shape[0] for x in part) // query_count
    depth = sum(x.shape[0] for x in rest)
    best, marks, _ = call(
        functools.partial(score_body, per_list, id_rows, first),
        [
            jax.ShapeDtypeStruct((total_lists // 2, width), F32),
            marks_shape,
            jax.ShapeDtypeStruct(grouped.shape, BF16),
        ],
        list_fill,
        list_rows,
        sources,
        old_marks,
        old_ranks,
        grouped,
        *rest,
        specs=[SMEM, VMEM, SMEM] + [VMEM] * (3 + len(rest)),
        scratch=[
            pltpu.VMEM((total_lists, width), jnp.int32),
            working(depth)[0],
            pltpu.VMEM((list_count, per_list), F32),
            *working(depth)[1:],
        ],
        alias={5: 2},
        limit=28,
        name="score",
    )
    got = lax.all_to_all(
        best.reshape(group, list_count // 2, width), AXES, split_axis=0, concat_axis=0, tiled=True
    )
    dup_max = call(
        functools.partial(pick_body, list_count),
        jax.ShapeDtypeStruct((probe_count, query_count), F32),
        got.reshape(total_lists // 2, width),
        probes.T,
        specs=[VMEM, VMEM],
        name="pick",
    )

    codes, scales, new_sums = call(
        functools.partial(append_body, list_count, slots),
        [
            jax.ShapeDtypeStruct((list_count, slots, dim), BF16),
            jax.ShapeDtypeStruct((list_count, slots), F32),
            jax.ShapeDtypeStruct((list_count, dim), F32),
        ],
        sources,
        old_marks,
        marks,
        centroids,
        list_sums,
        *chunks,
        specs=[SMEM] + [VMEM] * (4 + len(chunks)),
        scratch=[pltpu.VMEM((total_lists, width), jnp.int32), pltpu.VMEM((list_count * slots, max(x.shape[0] for x in chunks)), BF16)],
        name="append",
    )
    return dup_max.T, codes, scales, new_sums


def solution(mesh):
    split = P(AXES, None)
    return jax.shard_map(
        local,
        mesh=mesh,
        in_specs=(split, split, P(AXES), P(AXES, None, None), P(AXES), split, split),
        out_specs=(split, P(AXES, None, None), split, split),
        check_vma=False,
    )
```

```python
import functools

import jax
import jax.numpy as jnp
from jax import lax
from jax.experimental import pallas as pl
from jax.experimental.pallas import tpu as pltpu
from jax.sharding import PartitionSpec as P

AXES = ("lr", "lc")
VMEM = pl.BlockSpec(memory_space=pltpu.VMEM)
SMEM = pl.BlockSpec(memory_space=pltpu.SMEM)
BF16 = jnp.bfloat16
F32 = jnp.float32
LISTS_A_STEP = 4


def call(body, out_shape, *args, specs, name, scratch=(), flops=0, limit=24, alias=None):
    many = isinstance(out_shape, (list, tuple))
    return pl.pallas_call(
        body,
        in_specs=list(specs),
        out_specs=[VMEM] * len(out_shape) if many else VMEM,
        out_shape=out_shape,
        scratch_shapes=list(scratch),
        input_output_aliases=alias or {},
        compiler_params=pltpu.CompilerParams(vmem_limit_bytes=limit * 2**20),
        cost_estimate=pl.CostEstimate(flops=flops, bytes_accessed=0, transcendentals=0),
        name=name,
    )(*args)


def iota(shape, dim):
    return lax.broadcasted_iota(jnp.int32, shape, dim)


def over(x, n):
    if n & (n - 1):
        return x // n, x % n
    return x >> (n.bit_length() - 1), x & (n - 1)


def unpack(q_refs, src_ref, first, list_count, id_rows, dim, marks_ref):
    half = marks_ref.shape[1] // 2
    me = src_ref[src_ref.shape[0] - 1]
    marks_ref[...] = jnp.zeros(marks_ref.shape, F32)
    lists = iota((list_count, 2 * half), 0)
    lane = iota((list_count, 2 * half), 1)
    for q_ref in q_refs:
        for p in range(q_ref.shape[0] // (2 * half)):
            ids = q_ref[p * 2 * half : (p + 1) * 2 * half, dim:].astype(F32).T
            owners, places = ids[:id_rows], ids[ids.shape[0] // 2 : ids.shape[0] // 2 + id_rows]
            places = jnp.where(owners == me.astype(F32), places, -1.0).astype(jnp.int32)
            probed = jnp.zeros(lists.shape, jnp.int32)
            for l in range(list_count):
                hit = jnp.where(places[: id_rows - 1] == l, 1, 0)
                probed = jnp.where(lists == l, jnp.max(hit, axis=0, keepdims=True), probed)
            probed = probed.astype(F32)
            appended = jnp.where(places[id_rows - 1 :] == lists, 1.0, 0.0)
            turned = [pltpu.roll(x, half, 1) for x in (probed, appended)]
            for i, block in enumerate(
                (jnp.where(lane < half, probed, turned[1]), jnp.where(lane < half, turned[0], appended))
            ):
                start = pl.multiple_of(src_ref[first] * list_count, list_count)
                marks_ref[pl.ds(start, list_count), :] = block
                first += 1


def rank_marks(list_count, marks, past=None):
    rows, width = marks.shape
    half = width // 2
    a, b = iota((width, width), 0), iota((width, width), 1)
    same = over(a, half)[0] == over(b, half)[0]
    earlier = jnp.where(same & (a < b), 1.0, 0.0).astype(BF16)
    every = jnp.where(same, 1.0, 0.0).astype(BF16)
    r, s = iota((rows, rows), 0), iota((rows, rows), 1)
    alike = over(r, list_count)[1] == over(s, list_count)[1]
    before = jnp.where(alike & (s < r), 1.0, 0.0).astype(BF16)

    def counts(x):
        return jnp.dot(x.astype(BF16), every, preferred_element_type=F32).astype(BF16)

    place = jnp.dot(marks.astype(BF16), earlier, preferred_element_type=F32)
    place = place + jnp.dot(before, counts(marks), preferred_element_type=F32)
    if past is not None:
        place = place + jnp.dot(
            jnp.where(alike, 1.0, 0.0).astype(BF16), counts(past), preferred_element_type=F32
        )
    return jnp.where(marks > 0.5, place, -1.0).astype(jnp.int32)


def pair_ranks(ranks_ref, src_ref, first, list_count, half, part):
    blocks = []
    for i in range(2):
        start = pl.multiple_of(src_ref[first + i] * list_count, list_count)
        block = ranks_ref[pl.ds(start, list_count), :]
        blocks.append(block if i == part else pltpu.roll(block, half, 1))
    lane = iota(blocks[0].shape, 1)
    return jnp.where(lane < half, blocks[0], blocks[1])


def group_into(list_count, per_list, first_piece, src_ref, ranks_ref, old, q_refs, out_ref, pick, pairs_ref, starts):
    half = ranks_ref.shape[1] // 2
    depth = pick.shape[1]
    dim = out_ref.shape[1]
    lists_a_step = LISTS_A_STEP
    block = pick.shape[0] // lists_a_step
    pair_count = depth // (2 * half)
    lowest = highest = None
    for p in range(pair_count):
        ranks = pair_ranks(ranks_ref, src_ref, first_piece + 2 * p, list_count, half, 0)
        pairs_ref[p * list_count : (p + 1) * list_count, :] = ranks
        low = jnp.where(ranks < 0, per_list, ranks)
        lowest = low if p == 0 else jnp.minimum(lowest, low)
        highest = ranks if p == 0 else jnp.maximum(highest, ranks)
    low = jnp.min(lowest, axis=1, keepdims=True)
    low = jnp.minimum(low - (low & 15), per_list - block) if old else jnp.zeros_like(low)
    high = jnp.max(highest, axis=1, keepdims=True)
    beyond = sum((high >= low + k * block).astype(jnp.int32) for k in range(1, -(-per_list // block)))
    firsts = []
    for l in range(list_count):
        firsts.append(low[l, 0] if old else 0)
        starts[l] = firsts[l]
        starts[list_count + l] = beyond[l, 0]
    place = iota((block, 2 * half), 0).astype(BF16)
    one, none = jnp.ones(place.shape, BF16), jnp.zeros(place.shape, BF16)

    def product(count):
        total = None
        at = 0
        for q_ref in q_refs:
            n = q_ref.shape[0]
            term = jnp.dot(pick[:count, at : at + n], q_ref[:, :dim], preferred_element_type=F32)
            total = term if total is None else total + term
            at += n
        return total.astype(BF16)

    for step in range(list_count // lists_a_step):
        for i in range(lists_a_step):
            l = step * lists_a_step + i
            for p in range(pair_count):
                ranks = pairs_ref[p * list_count + l : p * list_count + l + 1, :] - firsts[l]
                pick[i * block : (i + 1) * block, p * 2 * half : (p + 1) * 2 * half] = jnp.where(
                    ranks.astype(F32).astype(BF16) == place, one, none
                )
        total = product(pick.shape[0])
        for i in range(lists_a_step):
            l = step * lists_a_step + i
            rows = pl.ds(pl.multiple_of(l * per_list + firsts[l], 16), block)
            part = total[i * block : (i + 1) * block]
            out_ref[rows, :] = out_ref[rows, :] + part if old else part
            if not old:
                out_ref[l * per_list + block : (l + 1) * per_list, :] = jnp.zeros((per_list - block, dim), BF16)

    @pl.loop(0, list_count)
    def _(l):
        @pl.loop(1, starts[list_count + l] + 1)
        def _(k):
            low = starts[l] + k * block
            first = jnp.minimum(low, per_list - block)
            for p in range(pair_count):
                ranks = pairs_ref[pl.ds(p * list_count + l, 1), :]
                ranks = jnp.where(ranks >= low, ranks - first, -1)
                pick[:block, p * 2 * half : (p + 1) * 2 * half] = jnp.where(
                    ranks.astype(F32).astype(BF16) == place, one, none
                )
            rows = pl.ds(pl.multiple_of(l * per_list + first, 16), block)
            out_ref[rows, :] = out_ref[rows, :] + product(block)


def group_body(list_count, per_list, id_rows, first_piece, src_ref, *refs):
    old, q_refs = (refs[:3], refs[3:-6]) if first_piece else (None, refs[:-6])
    out_ref, marks_ref, ranks_ref, pick, pairs, starts = refs[-6:]
    unpack(q_refs, src_ref, first_piece, list_count, id_rows, out_ref.shape[1], marks_ref)
    ranks_ref[...] = rank_marks(list_count, marks_ref[...], old[1][...] if old else None)
    group_into(
        list_count, per_list, first_piece, src_ref, ranks_ref, bool(old), q_refs, out_ref, pick, pairs, starts
    )
    if old:
        marks_ref[...] = marks_ref[...] + old[1][...]
        ranks_ref[...] = jnp.maximum(ranks_ref[...], old[2][...])


def score_body(per_list, id_rows, first_piece, fill_ref, rows, src_ref, old_marks_ref, old_ranks_ref, _, *refs):
    q_refs, (out_ref, marks_ref, grouped_ref, ranks_ref, pick, best, pairs, starts) = refs[:-8], refs[-8:]
    list_count, _, dim = rows.shape
    width = out_ref.shape[1]
    senders = ranks_ref.shape[0] // list_count
    unpack(q_refs, src_ref, first_piece, list_count, id_rows, dim, marks_ref)
    ranks_ref[...] = rank_marks(list_count, marks_ref[...], old_marks_ref[...])
    group_into(list_count, per_list, first_piece, src_ref, ranks_ref, True, q_refs, grouped_ref, pick, pairs, starts)
    for l in range(list_count):
        scores = lax.dot_general(
            rows[l],
            grouped_ref[l * per_list : (l + 1) * per_list, :],
            (((1,), (1,)), ((), ())),
            preferred_element_type=F32,
        )
        scores = jnp.where(iota(scores.shape, 0) < fill_ref[l], scores, -jnp.inf)
        best[l : l + 1, :] = jnp.max(scores, axis=0, keepdims=True)
    for s in range(senders):
        at = slice(s * list_count, (s + 1) * list_count)
        ranks = jnp.maximum(ranks_ref[at, :], old_ranks_ref[at, :])
        found = jnp.zeros(ranks.shape, F32)
        for c in range(per_list // width):
            index = jnp.clip(ranks - c * width, 0, width - 1)
            got = jnp.take_along_axis(best[:, c * width : (c + 1) * width], index, axis=1)
            found = jnp.where((ranks >= c * width) & (ranks < (c + 1) * width), got, found)
        lane = iota((list_count // 2, width), 1)
        turned = pltpu.roll(found, width // 2, 1)
        packed = jnp.where(lane < width // 2, found[: list_count // 2], turned[list_count // 2 :])
        out_ref[s * (list_count // 2) : (s + 1) * (list_count // 2), :] = packed


def pick_body(list_count, got_ref, ids_ref, out_ref):
    probe_count, count = ids_ref.shape
    half = list_count // 2
    owner, place = over(ids_ref[...], list_count)
    second = jnp.where(place >= half, 1, 0)
    row = owner * half + place - second * half
    rows = iota(got_ref.shape, 0)
    row = jnp.concatenate([jnp.where(second == 0, row, -1), jnp.where(second == 1, row, -1)], axis=1)
    got = got_ref[...]
    found = []
    for j in range(probe_count):
        found.append(jnp.sum(jnp.where(rows == row[j : j + 1, :], got, 0.0), axis=0, keepdims=True))
    found = jnp.concatenate(found, axis=0)
    out_ref[...] = found[:, :count] + found[:, count:]


def append_body(list_count, slots, src_ref, old_marks_ref, marks_ref, center_ref, sums_ref, *refs):
    q_refs, (codes_ref, scales_ref, sums_out_ref, ranks_ref, pick) = refs[:-5], refs[-5:]
    ranks_ref[...] = rank_marks(list_count, old_marks_ref[...] + marks_ref[...])
    half = ranks_ref.shape[1] // 2
    dim = center_ref.shape[1]
    place = iota((slots, 2 * half), 0)
    piece = 0
    total = jnp.zeros((list_count * slots, dim), F32)
    live = jnp.zeros((list_count * slots, 1), F32)
    for q_ref in q_refs:
        n = q_ref.shape[0]
        for p in range(n // (2 * half)):
            ranks = pair_ranks(ranks_ref, src_ref, piece, list_count, half, 1)
            piece += 2
            for l in range(list_count):
                hit = jnp.where(ranks[l : l + 1, :] == place, 1.0, 0.0)
                pick[l * slots : (l + 1) * slots, p * 2 * half : (p + 1) * 2 * half] = hit.astype(BF16)
        chosen = pick[:, :n]
        live = live + jnp.sum(chosen.astype(F32), axis=1, keepdims=True)
        total = total + jnp.dot(chosen, q_ref[:, :dim], preferred_element_type=F32)
    for l in range(list_count):
        rows = slice(l * slots, (l + 1) * slots)
        used = live[rows, :] > 0.5
        residual = jnp.where(used, total[rows, :] - center_ref[l : l + 1, :], 0.0)
        scale = jnp.max(jnp.abs(residual), axis=1, keepdims=True) + 1e-6
        codes_ref[l] = (residual / scale).astype(BF16)
        scales_ref[l : l + 1, :] = jnp.where(used, scale, 0.0).T
        sums_out_ref[l : l + 1, :] = sums_ref[l : l + 1, :] + jnp.sum(residual, axis=0, keepdims=True)


def swap_pairs(rows, cols, of):
    pairs = []
    for lr in range(rows):
        for lc in range(cols):
            to = of(lr, lc)
            pairs.append((lr * cols + lc, to[0] * cols + to[1]))
    return pairs


def after(x, *others):
    return lax.optimization_barrier((x, *others))[0]


def swap_core(x, rows, cols):
    return lax.ppermute(x, AXES, swap_pairs(rows, cols, lambda r, c: (r ^ 1, c)))


def gather_queries(queries, rows, cols, group_early):
    me = lax.axis_index(AXES)
    if (rows, cols) != (8, 4):
        whole = lax.all_gather(queries, AXES, axis=0, tiled=True)
        half = whole.shape[0] // 2
        sources = jnp.append(jnp.arange(rows * cols, dtype=jnp.int32), me)
        return [whole[:half]], [whole[half:]], sources, group_early(sources, [whole[:half]])

    def send(x, of):
        return lax.ppermute(x, AXES, swap_pairs(rows, cols, of))

    def first(x):
        return jnp.concatenate([x, send(x, lambda r, c: (r ^ (4 if r & 1 else 2), c))], 0)

    def second(x):
        return jnp.concatenate([x, send(x, lambda r, c: (r ^ (2 if r & 1 else 4), c))], 0)

    def other(x):
        return [x, swap_core(x, rows, cols)]

    r, c = lax.axis_index("lr"), lax.axis_index("lc")
    sources = []
    for planes in ((0, 1), (2, 3)):
        for core in (0, 1):
            odd = (r ^ core) & 1
            one, two = jnp.where(odd == 1, 4, 2), jnp.where(odd == 1, 2, 4)
            for hops in range(4):
                row = r ^ core
                row = row ^ one if hops & 1 else row
                row = row ^ two if hops & 2 else row
                sources += [row * cols + (c ^ plane) for plane in planes]
    sources = jnp.stack(sources + [me]).astype(jnp.int32)

    z1, z2, z3 = (send(queries, lambda r, c, k=k: (r, c ^ k)) for k in (1, 2, 3))
    pair = jnp.concatenate([queries, z1], 0)
    far = jnp.concatenate([z2, z3], 0)
    near = second(first(pair))
    far = second(first(far))
    pieces = near.shape[0] // queries.shape[0]
    half = group_early(sources, [near])
    part = other(after(near, *half))
    part[0] = near
    grouped = group_early(sources, part[1:], pieces, tuple(half))
    return part, other(far), sources, grouped


def local(queries, probes, assign, list_rows, list_fill, centroids, list_sums):
    rows, cols = lax.axis_size("lr"), lax.axis_size("lc")
    group = rows * cols
    list_count, row_count, dim = list_rows.shape
    query_count, probe_count = probes.shape
    pair_cap = 2 * query_count * probe_count // group
    append_cap = max(2, 2 * query_count // group)
    per_list = group * pair_cap // list_count
    slots = group * append_cap // list_count
    width = 2 * query_count
    total_lists = group * list_count

    ids = jnp.concatenate([probes, assign[:, None]], axis=1)
    id_rows = probe_count + 1
    id_lanes = 64
    spare = jnp.zeros((query_count, id_lanes - id_rows), jnp.int32)
    digits = jnp.concatenate([ids // list_count, spare, ids % list_count, spare], axis=1)
    packed = jnp.concatenate([queries, digits.astype(BF16)], axis=1)

    marks_shape = jax.ShapeDtypeStruct((total_lists, width), F32)
    ranks_shape = jax.ShapeDtypeStruct((total_lists, width), jnp.int32)

    def working(depth):
        share = -(-per_list * depth // (group * query_count * 16)) * 16
        return [
            pltpu.VMEM((LISTS_A_STEP * min(per_list, share + 16), depth), BF16),
            pltpu.VMEM((depth // width * list_count, width), jnp.int32),
            pltpu.SMEM((2 * list_count,), jnp.int32),
        ]

    def group_early(sources, part, first=0, old=()):
        depth = sum(x.shape[0] for x in part)
        return call(
            functools.partial(group_body, list_count, per_list, id_rows, first),
            [jax.ShapeDtypeStruct((list_count * per_list, dim), BF16), marks_shape, ranks_shape],
            sources,
            *old,
            *part,
            specs=[SMEM] + [VMEM] * (len(old) + len(part)),
            scratch=working(depth),
            flops=2 * list_count * per_list * depth * dim,
            limit=28,
            alias={1: 0} if old else None,
            name="group",
        )

    part, rest, sources, (grouped, old_marks, old_ranks) = gather_queries(packed, rows, cols, group_early)
    chunks = part + rest
    first = sum(x.shape[0] for x in part) // query_count
    depth = sum(x.shape[0] for x in rest)
    best, marks, _ = call(
        functools.partial(score_body, per_list, id_rows, first),
        [
            jax.ShapeDtypeStruct((total_lists // 2, width), F32),
            marks_shape,
            jax.ShapeDtypeStruct(grouped.shape, BF16),
        ],
        list_fill,
        list_rows,
        sources,
        old_marks,
        old_ranks,
        grouped,
        *rest,
        specs=[SMEM, VMEM, SMEM] + [VMEM] * (3 + len(rest)),
        scratch=[
            pltpu.VMEM((total_lists, width), jnp.int32),
            working(depth)[0],
            pltpu.VMEM((list_count, per_list), F32),
            *working(depth)[1:],
        ],
        alias={5: 2},
        limit=28,
        name="score",
    )
    got = lax.all_to_all(
        best.reshape(group, list_count // 2, width), AXES, split_axis=0, concat_axis=0, tiled=True
    )
    dup_max = call(
        functools.partial(pick_body, list_count),
        jax.ShapeDtypeStruct((probe_count, query_count), F32),
        got.reshape(total_lists // 2, width),
        probes.T,
        specs=[VMEM, VMEM],
        name="pick",
    )

    codes, scales, new_sums = call(
        functools.partial(append_body, list_count, slots),
        [
            jax.ShapeDtypeStruct((list_count, slots, dim), BF16),
            jax.ShapeDtypeStruct((list_count, slots), F32),
            jax.ShapeDtypeStruct((list_count, dim), F32),
        ],
        sources,
        old_marks,
        marks,
        centroids,
        list_sums,
        *chunks,
        specs=[SMEM] + [VMEM] * (4 + len(chunks)),
        scratch=[pltpu.VMEM((total_lists, width), jnp.int32), pltpu.VMEM((list_count * slots, max(x.shape[0] for x in chunks)), BF16)],
        name="append",
    )
    return dup_max.T, codes, scales, new_sums


def solution(mesh):
    split = P(AXES, None)
    return jax.shard_map(
        local,
        mesh=mesh,
        in_specs=(split, split, P(AXES), P(AXES, None, None), P(AXES), split, split),
        out_specs=(split, P(AXES, None, None), split, split),
        check_vma=False,
    )
```

```python
import functools

import jax
import jax.numpy as jnp
from jax import lax
from jax.experimental import pallas as pl
from jax.experimental.pallas import tpu as pltpu
from jax.sharding import PartitionSpec as P

AXES = ("lr", "lc")
VMEM = pl.BlockSpec(memory_space=pltpu.VMEM)
SMEM = pl.BlockSpec(memory_space=pltpu.SMEM)
BF16 = jnp.bfloat16
F32 = jnp.float32
LISTS_A_STEP = 8


def call(body, out_shape, *args, specs, name, scratch=(), flops=0, limit=24, alias=None):
    many = isinstance(out_shape, (list, tuple))
    return pl.pallas_call(
        body,
        in_specs=list(specs),
        out_specs=[VMEM] * len(out_shape) if many else VMEM,
        out_shape=out_shape,
        scratch_shapes=list(scratch),
        input_output_aliases=alias or {},
        compiler_params=pltpu.CompilerParams(vmem_limit_bytes=limit * 2**20),
        cost_estimate=pl.CostEstimate(flops=flops, bytes_accessed=0, transcendentals=0),
        name=name,
    )(*args)


def iota(shape, dim):
    return lax.broadcasted_iota(jnp.int32, shape, dim)


def over(x, n):
    if n & (n - 1):
        return x // n, x % n
    return x >> (n.bit_length() - 1), x & (n - 1)


def unpack(q_refs, src_ref, first, list_count, id_rows, dim, marks_ref):
    half = marks_ref.shape[1] // 2
    me = src_ref[src_ref.shape[0] - 1]
    marks_ref[...] = jnp.zeros(marks_ref.shape, F32)
    lists = iota((list_count, 2 * half), 0)
    lane = iota((list_count, 2 * half), 1)
    for q_ref in q_refs:
        for p in range(q_ref.shape[0] // (2 * half)):
            ids = q_ref[p * 2 * half : (p + 1) * 2 * half, dim:].astype(F32).T
            owners, places = ids[:id_rows], ids[ids.shape[0] // 2 : ids.shape[0] // 2 + id_rows]
            places = jnp.where(owners == me.astype(F32), places, -1.0).astype(jnp.int32)
            probed = jnp.zeros(lists.shape, jnp.int32)
            for l in range(list_count):
                hit = jnp.where(places[: id_rows - 1] == l, 1, 0)
                probed = jnp.where(lists == l, jnp.max(hit, axis=0, keepdims=True), probed)
            probed = probed.astype(F32)
            appended = jnp.where(places[id_rows - 1 :] == lists, 1.0, 0.0)
            turned = [pltpu.roll(x, half, 1) for x in (probed, appended)]
            for i, block in enumerate(
                (jnp.where(lane < half, probed, turned[1]), jnp.where(lane < half, turned[0], appended))
            ):
                start = pl.multiple_of(src_ref[first] * list_count, list_count)
                marks_ref[pl.ds(start, list_count), :] = block
                first += 1


def rank_marks(list_count, marks, past=None):
    rows, width = marks.shape
    half = width // 2
    a, b = iota((width, width), 0), iota((width, width), 1)
    same = over(a, half)[0] == over(b, half)[0]
    earlier = jnp.where(same & (a < b), 1.0, 0.0).astype(BF16)
    every = jnp.where(same, 1.0, 0.0).astype(BF16)
    r, s = iota((rows, rows), 0), iota((rows, rows), 1)
    alike = over(r, list_count)[1] == over(s, list_count)[1]
    before = jnp.where(alike & (s < r), 1.0, 0.0).astype(BF16)

    def counts(x):
        return jnp.dot(x.astype(BF16), every, preferred_element_type=F32).astype(BF16)

    place = jnp.dot(marks.astype(BF16), earlier, preferred_element_type=F32)
    place = place + jnp.dot(before, counts(marks), preferred_element_type=F32)
    if past is not None:
        place = place + jnp.dot(
            jnp.where(alike, 1.0, 0.0).astype(BF16), counts(past), preferred_element_type=F32
        )
    return jnp.where(marks > 0.5, place, -1.0).astype(jnp.int32)


def pair_ranks(ranks_ref, src_ref, first, list_count, half, part):
    blocks = []
    for i in range(2):
        start = pl.multiple_of(src_ref[first + i] * list_count, list_count)
        block = ranks_ref[pl.ds(start, list_count), :]
        blocks.append(block if i == part else pltpu.roll(block, half, 1))
    lane = iota(blocks[0].shape, 1)
    return jnp.where(lane < half, blocks[0], blocks[1])


def group_into(list_count, per_list, first_piece, src_ref, ranks_ref, old, q_refs, out_ref, pick, pairs_ref, starts):
    half = ranks_ref.shape[1] // 2
    depth = pick.shape[1]
    dim = out_ref.shape[1]
    lists_a_step = LISTS_A_STEP
    block = pick.shape[0] // lists_a_step
    pair_count = depth // (2 * half)
    lowest = highest = None
    for p in range(pair_count):
        ranks = pair_ranks(ranks_ref, src_ref, first_piece + 2 * p, list_count, half, 0)
        pairs_ref[p * list_count : (p + 1) * list_count, :] = ranks
        low = jnp.where(ranks < 0, per_list, ranks)
        lowest = low if p == 0 else jnp.minimum(lowest, low)
        highest = ranks if p == 0 else jnp.maximum(highest, ranks)
    low = jnp.min(lowest, axis=1, keepdims=True)
    low = jnp.minimum(low - (low & 15), per_list - block) if old else jnp.zeros_like(low)
    high = jnp.max(highest, axis=1, keepdims=True)
    beyond = sum((high >= low + k * block).astype(jnp.int32) for k in range(1, -(-per_list // block)))
    firsts = []
    for l in range(list_count):
        firsts.append(low[l, 0] if old else 0)
        starts[l] = firsts[l]
        starts[list_count + l] = beyond[l, 0]
    place = iota((block, 2 * half), 0).astype(BF16)
    one, none = jnp.ones(place.shape, BF16), jnp.zeros(place.shape, BF16)

    def product(count):
        total = None
        at = 0
        for q_ref in q_refs:
            n = q_ref.shape[0]
            term = jnp.dot(pick[:count, at : at + n], q_ref[:, :dim], preferred_element_type=F32)
            total = term if total is None else total + term
            at += n
        return total.astype(BF16)

    for step in range(list_count // lists_a_step):
        for i in range(lists_a_step):
            l = step * lists_a_step + i
            for p in range(pair_count):
                ranks = pairs_ref[p * list_count + l : p * list_count + l + 1, :] - firsts[l]
                pick[i * block : (i + 1) * block, p * 2 * half : (p + 1) * 2 * half] = jnp.where(
                    ranks.astype(F32).astype(BF16) == place, one, none
                )
        total = product(pick.shape[0])
        for i in range(lists_a_step):
            l = step * lists_a_step + i
            rows = pl.ds(pl.multiple_of(l * per_list + firsts[l], 16), block)
            part = total[i * block : (i + 1) * block]
            out_ref[rows, :] = out_ref[rows, :] + part if old else part
            if not old:
                out_ref[l * per_list + block : (l + 1) * per_list, :] = jnp.zeros((per_list - block, dim), BF16)

    @pl.loop(0, list_count)
    def _(l):
        @pl.loop(1, starts[list_count + l] + 1)
        def _(k):
            low = starts[l] + k * block
            first = jnp.minimum(low, per_list - block)
            for p in range(pair_count):
                ranks = pairs_ref[pl.ds(p * list_count + l, 1), :]
                ranks = jnp.where(ranks >= low, ranks - first, -1)
                pick[:block, p * 2 * half : (p + 1) * 2 * half] = jnp.where(
                    ranks.astype(F32).astype(BF16) == place, one, none
                )
            rows = pl.ds(pl.multiple_of(l * per_list + first, 16), block)
            out_ref[rows, :] = out_ref[rows, :] + product(block)


def group_body(list_count, per_list, id_rows, first_piece, src_ref, *refs):
    old, q_refs = (refs[:3], refs[3:-6]) if first_piece else (None, refs[:-6])
    out_ref, marks_ref, ranks_ref, pick, pairs, starts = refs[-6:]
    unpack(q_refs, src_ref, first_piece, list_count, id_rows, out_ref.shape[1], marks_ref)
    ranks_ref[...] = rank_marks(list_count, marks_ref[...], old[1][...] if old else None)
    group_into(
        list_count, per_list, first_piece, src_ref, ranks_ref, bool(old), q_refs, out_ref, pick, pairs, starts
    )
    if old:
        marks_ref[...] = marks_ref[...] + old[1][...]
        ranks_ref[...] = jnp.maximum(ranks_ref[...], old[2][...])


def score_body(per_list, id_rows, first_piece, fill_ref, rows, src_ref, old_marks_ref, old_ranks_ref, _, *refs):
    q_refs, (out_ref, marks_ref, grouped_ref, ranks_ref, pick, best, pairs, starts) = refs[:-8], refs[-8:]
    list_count, _, dim = rows.shape
    width = out_ref.shape[1]
    senders = ranks_ref.shape[0] // list_count
    unpack(q_refs, src_ref, first_piece, list_count, id_rows, dim, marks_ref)
    ranks_ref[...] = rank_marks(list_count, marks_ref[...], old_marks_ref[...])
    group_into(list_count, per_list, first_piece, src_ref, ranks_ref, True, q_refs, grouped_ref, pick, pairs, starts)
    for l in range(list_count):
        scores = lax.dot_general(
            rows[l],
            grouped_ref[l * per_list : (l + 1) * per_list, :],
            (((1,), (1,)), ((), ())),
            preferred_element_type=F32,
        )
        scores = jnp.where(iota(scores.shape, 0) < fill_ref[l], scores, -jnp.inf)
        best[l : l + 1, :] = jnp.max(scores, axis=0, keepdims=True)
    for s in range(senders):
        at = slice(s * list_count, (s + 1) * list_count)
        ranks = jnp.maximum(ranks_ref[at, :], old_ranks_ref[at, :])
        found = jnp.zeros(ranks.shape, F32)
        for c in range(per_list // width):
            index = jnp.clip(ranks - c * width, 0, width - 1)
            got = jnp.take_along_axis(best[:, c * width : (c + 1) * width], index, axis=1)
            found = jnp.where((ranks >= c * width) & (ranks < (c + 1) * width), got, found)
        lane = iota((list_count // 2, width), 1)
        turned = pltpu.roll(found, width // 2, 1)
        packed = jnp.where(lane < width // 2, found[: list_count // 2], turned[list_count // 2 :])
        out_ref[s * (list_count // 2) : (s + 1) * (list_count // 2), :] = packed


def pick_body(list_count, got_ref, ids_ref, out_ref):
    probe_count, count = ids_ref.shape
    half = list_count // 2
    owner, place = over(ids_ref[...], list_count)
    second = jnp.where(place >= half, 1, 0)
    row = owner * half + place - second * half
    rows = iota(got_ref.shape, 0)
    row = jnp.concatenate([jnp.where(second == 0, row, -1), jnp.where(second == 1, row, -1)], axis=1)
    got = got_ref[...]
    found = []
    for j in range(probe_count):
        found.append(jnp.sum(jnp.where(rows == row[j : j + 1, :], got, 0.0), axis=0, keepdims=True))
    found = jnp.concatenate(found, axis=0)
    out_ref[...] = found[:, :count] + found[:, count:]


def append_body(list_count, slots, src_ref, old_marks_ref, marks_ref, center_ref, sums_ref, *refs):
    q_refs, (codes_ref, scales_ref, sums_out_ref, ranks_ref, pick) = refs[:-5], refs[-5:]
    ranks_ref[...] = rank_marks(list_count, old_marks_ref[...] + marks_ref[...])
    half = ranks_ref.shape[1] // 2
    dim = center_ref.shape[1]
    place = iota((slots, 2 * half), 0)
    piece = 0
    total = jnp.zeros((list_count * slots, dim), F32)
    live = jnp.zeros((list_count * slots, 1), F32)
    for q_ref in q_refs:
        n = q_ref.shape[0]
        for p in range(n // (2 * half)):
            ranks = pair_ranks(ranks_ref, src_ref, piece, list_count, half, 1)
            piece += 2
            for l in range(list_count):
                hit = jnp.where(ranks[l : l + 1, :] == place, 1.0, 0.0)
                pick[l * slots : (l + 1) * slots, p * 2 * half : (p + 1) * 2 * half] = hit.astype(BF16)
        chosen = pick[:, :n]
        live = live + jnp.sum(chosen.astype(F32), axis=1, keepdims=True)
        total = total + jnp.dot(chosen, q_ref[:, :dim], preferred_element_type=F32)
    for l in range(list_count):
        rows = slice(l * slots, (l + 1) * slots)
        used = live[rows, :] > 0.5
        residual = jnp.where(used, total[rows, :] - center_ref[l : l + 1, :], 0.0)
        scale = jnp.max(jnp.abs(residual), axis=1, keepdims=True) + 1e-6
        codes_ref[l] = (residual / scale).astype(BF16)
        scales_ref[l : l + 1, :] = jnp.where(used, scale, 0.0).T
        sums_out_ref[l : l + 1, :] = sums_ref[l : l + 1, :] + jnp.sum(residual, axis=0, keepdims=True)


def swap_pairs(rows, cols, of):
    pairs = []
    for lr in range(rows):
        for lc in range(cols):
            to = of(lr, lc)
            pairs.append((lr * cols + lc, to[0] * cols + to[1]))
    return pairs


def after(x, *others):
    return lax.optimization_barrier((x, *others))[0]


def swap_core(x, rows, cols):
    return lax.ppermute(x, AXES, swap_pairs(rows, cols, lambda r, c: (r ^ 1, c)))


def gather_queries(queries, rows, cols, group_early):
    me = lax.axis_index(AXES)
    if (rows, cols) != (8, 4):
        whole = lax.all_gather(queries, AXES, axis=0, tiled=True)
        half = whole.shape[0] // 2
        sources = jnp.append(jnp.arange(rows * cols, dtype=jnp.int32), me)
        return [whole[:half]], [whole[half:]], sources, group_early(sources, [whole[:half]])

    def send(x, of):
        return lax.ppermute(x, AXES, swap_pairs(rows, cols, of))

    def first(x):
        return jnp.concatenate([x, send(x, lambda r, c: (r ^ (4 if r & 1 else 2), c))], 0)

    def second(x):
        return jnp.concatenate([x, send(x, lambda r, c: (r ^ (2 if r & 1 else 4), c))], 0)

    def other(x):
        return [x, swap_core(x, rows, cols)]

    r, c = lax.axis_index("lr"), lax.axis_index("lc")
    sources = []
    for planes in ((0, 1), (2, 3)):
        for core in (0, 1):
            odd = (r ^ core) & 1
            one, two = jnp.where(odd == 1, 4, 2), jnp.where(odd == 1, 2, 4)
            for hops in range(4):
                row = r ^ core
                row = row ^ one if hops & 1 else row
                row = row ^ two if hops & 2 else row
                sources += [row * cols + (c ^ plane) for plane in planes]
    sources = jnp.stack(sources + [me]).astype(jnp.int32)

    z1, z2, z3 = (send(queries, lambda r, c, k=k: (r, c ^ k)) for k in (1, 2, 3))
    pair = jnp.concatenate([queries, z1], 0)
    far = jnp.concatenate([z2, z3], 0)
    near = second(first(pair))
    far = second(first(far))
    pieces = near.shape[0] // queries.shape[0]
    half = group_early(sources, [near])
    part = other(after(near, *half))
    part[0] = near
    grouped = group_early(sources, part[1:], pieces, tuple(half))
    return part, other(far), sources, grouped


def local(queries, probes, assign, list_rows, list_fill, centroids, list_sums):
    rows, cols = lax.axis_size("lr"), lax.axis_size("lc")
    group = rows * cols
    list_count, row_count, dim = list_rows.shape
    query_count, probe_count = probes.shape
    pair_cap = 2 * query_count * probe_count // group
    append_cap = max(2, 2 * query_count // group)
    per_list = group * pair_cap // list_count
    slots = group * append_cap // list_count
    width = 2 * query_count
    total_lists = group * list_count

    ids = jnp.concatenate([probes, assign[:, None]], axis=1)
    id_rows = probe_count + 1
    id_lanes = 64
    spare = jnp.zeros((query_count, id_lanes - id_rows), jnp.int32)
    digits = jnp.concatenate([ids // list_count, spare, ids % list_count, spare], axis=1)
    packed = jnp.concatenate([queries, digits.astype(BF16)], axis=1)

    marks_shape = jax.ShapeDtypeStruct((total_lists, width), F32)
    ranks_shape = jax.ShapeDtypeStruct((total_lists, width), jnp.int32)

    def working(depth):
        share = -(-per_list * depth // (group * query_count * 16)) * 16
        return [
            pltpu.VMEM((LISTS_A_STEP * min(per_list, share + 16), depth), BF16),
            pltpu.VMEM((depth // width * list_count, width), jnp.int32),
            pltpu.SMEM((2 * list_count,), jnp.int32),
        ]

    def group_early(sources, part, first=0, old=()):
        depth = sum(x.shape[0] for x in part)
        return call(
            functools.partial(group_body, list_count, per_list, id_rows, first),
            [jax.ShapeDtypeStruct((list_count * per_list, dim), BF16), marks_shape, ranks_shape],
            sources,
            *old,
            *part,
            specs=[SMEM] + [VMEM] * (len(old) + len(part)),
            scratch=working(depth),
            flops=2 * list_count * per_list * depth * dim,
            limit=28,
            alias={1: 0} if old else None,
            name="group",
        )

    part, rest, sources, (grouped, old_marks, old_ranks) = gather_queries(packed, rows, cols, group_early)
    chunks = part + rest
    first = sum(x.shape[0] for x in part) // query_count
    depth = sum(x.shape[0] for x in rest)
    best, marks, _ = call(
        functools.partial(score_body, per_list, id_rows, first),
        [
            jax.ShapeDtypeStruct((total_lists // 2, width), F32),
            marks_shape,
            jax.ShapeDtypeStruct(grouped.shape, BF16),
        ],
        list_fill,
        list_rows,
        sources,
        old_marks,
        old_ranks,
        grouped,
        *rest,
        specs=[SMEM, VMEM, SMEM] + [VMEM] * (3 + len(rest)),
        scratch=[
            pltpu.VMEM((total_lists, width), jnp.int32),
            working(depth)[0],
            pltpu.VMEM((list_count, per_list), F32),
            *working(depth)[1:],
        ],
        alias={5: 2},
        limit=28,
        name="score",
    )
    got = lax.all_to_all(
        best.reshape(group, list_count // 2, width), AXES, split_axis=0, concat_axis=0, tiled=True
    )
    dup_max = call(
        functools.partial(pick_body, list_count),
        jax.ShapeDtypeStruct((probe_count, query_count), F32),
        got.reshape(total_lists // 2, width),
        probes.T,
        specs=[VMEM, VMEM],
        name="pick",
    )

    codes, scales, new_sums = call(
        functools.partial(append_body, list_count, slots),
        [
            jax.ShapeDtypeStruct((list_count, slots, dim), BF16),
            jax.ShapeDtypeStruct((list_count, slots), F32),
            jax.ShapeDtypeStruct((list_count, dim), F32),
        ],
        sources,
        old_marks,
        marks,
        centroids,
        list_sums,
        *chunks,
        specs=[SMEM] + [VMEM] * (4 + len(chunks)),
        scratch=[pltpu.VMEM((total_lists, width), jnp.int32), pltpu.VMEM((list_count * slots, max(x.shape[0] for x in chunks)), BF16)],
        name="append",
    )
    return dup_max.T, codes, scales, new_sums


def solution(mesh):
    split = P(AXES, None)
    return jax.shard_map(
        local,
        mesh=mesh,
        in_specs=(split, split, P(AXES), P(AXES, None, None), P(AXES), split, split),
        out_specs=(split, P(AXES, None, None), split, split),
        check_vma=False,
    )
```
